256 devices in a mesh: seq: 32 (over z, y), tensor: 8 (over x, core).
Axes of the slice: x: 4, y: 4, z: 8, core: 2. Of those that a mesh axis runs over, the one named last changes fastest.
Arguments:
- projections: bfloat16 [3, 8192, 8192], P(None, 'seq', 'tensor'), may hold values from -6 to 6
- out_grad: bfloat16 [8192, 8192], P('seq', 'tensor'), may hold values from -6 to 6
- short_filters: float32 [3, 7, 8192], P(None, None, 'tensor'), may hold values from -2 to 2
- long_filter: float32 [128, 8192], P('seq', 'tensor'), may hold values from -0.5 to 0.5
Outputs:
- grad_projections: bfloat16 [3, 8192, 8192], P(None, 'seq', 'tensor')
- grad_short: float32 [3, 7, 8192], P(None, None, 'tensor')
- grad_long: float32 [128, 8192], P('seq', 'tensor')
The draws below stay inside these ranges and needn't reach their ends.
All inputs are finite; a program needn't handle non-finite values.
Results may differ from the reference program's by a relative error of at most 0.006.
Values may be sent and summed in bfloat16 or wider, within the bound.
A program may use at most 64 MiB of HBM per device.

```python
import jax
import jax.numpy as jnp
from jax import lax

WIDTH = 8192
STAPS = 7
LTAPS = 128
TOKENS = 8192


def shard_levels(own_key, dims, cuts, least, top_value):
    gain, own = 1.0, jax.random.fold_in(own_key, 6)
    for dim, blocks in cuts:
        heights = jnp.exp(jax.random.uniform(jax.random.fold_in(own, dim), (blocks,), jnp.float32, least / len(cuts), top_value / len(cuts)))
        gain = gain * jnp.repeat(heights, dims[dim] // blocks).reshape([-1 if axis == dim else 1 for axis in range(len(dims))])
    return gain


def gaussian(rng, dims, scale, most, cuts=(), kind=jnp.bfloat16):
    drawn = jax.random.normal(rng, dims, jnp.float32) * scale
    if len(cuts) > 0:
        drawn = shard_levels(rng, dims, cuts, -0.22, 0.18) * drawn
    return jnp.clip(drawn, min=-most, max=most).astype(kind)


def setup_inputs(seed: int = 0) -> dict:
    splits = jax.random.split(jax.random.key(seed), 5)
    return {
        "projections": gaussian(splits[0], (3, TOKENS, WIDTH), 1.0, 6.0, ((1, 32), (2, 8))),
        "out_grad": gaussian(splits[1], (TOKENS, WIDTH), 1.0, 6.0, ((0, 32), (1, 8))),
        "short_filters": gaussian(splits[2], (3, STAPS, WIDTH), STAPS ** -0.5, 2.0, ((2, 8),), jnp.float32),
        "long_filter": gaussian(splits[3], (LTAPS, WIDTH), LTAPS ** -0.5, 0.5, ((0, 32), (1, 8)), jnp.float32),
    }


def correlate(extended, taps):
    tap_count = taps.shape[0]
    out_count = extended.shape[0] - tap_count + 1
    if tap_count <= out_count:
        def add_tap(index, total):
            index = jnp.asarray(index).astype(jnp.int32)
            window = lax.dynamic_slice_in_dim(extended, index, out_count, 0)
            weight = lax.dynamic_slice_in_dim(taps, index, 1, 0)
            return total + window * weight
        start = jnp.zeros((out_count, extended.shape[1]), extended.dtype)
        return lax.fori_loop(0, tap_count, add_tap, start)

    def one_output(index, total):
        index = jnp.asarray(index).astype(jnp.int32)
        window = lax.dynamic_slice_in_dim(extended, index, tap_count, 0)
        value = jnp.sum(window * taps, axis=0, keepdims=True)
        return lax.dynamic_update_slice_in_dim(total, value, index, 0)
    start = jnp.zeros((out_count, extended.shape[1]), extended.dtype)
    return lax.fori_loop(0, out_count, one_output, start)


def block_grads(pieces):
    inputs_bf, cotangent_bf, short_taps, long_taps = pieces
    inputs = inputs_bf.astype(jnp.float32)
    cotangent = cotangent_bf.astype(jnp.float32)
    short_len = short_taps.shape[1]
    long_len = long_taps.shape[0]
    inputs_ext = jnp.pad(inputs, ((0, 0), (short_len - 1, 0), (0, 0)))
    features = jax.vmap(correlate)(inputs_ext, short_taps[:, ::-1])
    gating = features[1] * features[2]
    history = jnp.pad(gating, ((long_len - 1, 0), (0, 0)))
    mixing = correlate(history, long_taps[::-1])
    grad_query = cotangent * mixing
    grad_mixing = cotangent * features[0]
    grad_gating = correlate(jnp.pad(grad_mixing, ((0, long_len - 1), (0, 0))), long_taps)
    grad_features = jnp.stack([grad_query, grad_gating * features[2], grad_gating * features[1]])
    grad_inputs = jax.vmap(correlate)(jnp.pad(grad_features, ((0, 0), (0, short_len - 1), (0, 0))), short_taps).astype(jnp.bfloat16)
    grad_short = jax.vmap(correlate)(inputs_ext, grad_features)[:, ::-1]
    grad_long = correlate(history, grad_mixing)[::-1]
    return grad_inputs, grad_short, grad_long


def split_blocks(array, block_count):
    block_width = array.shape[-1] // block_count
    return jnp.moveaxis(array.reshape(array.shape[:-1] + (block_count, block_width)), -2, 0)


def join_blocks(array):
    moved = jnp.moveaxis(array, 0, -2)
    return moved.reshape(moved.shape[:-2] + (moved.shape[-2] * moved.shape[-1],))


def reference(projections, out_grad, short_filters, long_filter):
    block_count = 8
    results = lax.map(block_grads, (split_blocks(projections, block_count), split_blocks(out_grad, block_count), split_blocks(short_filters, block_count), split_blocks(long_filter, block_count)))
    return join_blocks(results[0]), join_blocks(results[1]), join_blocks(results[2])
```

```python
import jax
import jax.numpy as jnp
import ml_dtypes
import numpy as np
from jax import lax
from jax.experimental import pallas as pl
from jax.experimental.pallas import tpu as pltpu
from jax.sharding import PartitionSpec as P

MESH = pl.DeviceIdType.MESH
F32 = jnp.float32
BF16 = jnp.bfloat16

STAPS = 7
LTAPS = 128
ROWS = 256
COLS = 1024
LANES = 128
CHUNKS = COLS // LANES
WIDE = 256
QUADS = COLS // WIDE
SEQ = 32
OWN_TAPS = LTAPS // SEQ
POINTS = ROWS + LTAPS
HALF = POINTS // 2
EDGE = 16
PIECES = 3 * CHUNKS


def transforms():
    freqs = 2.0 * np.pi * (np.arange(HALF) + 0.5) / POINTS

    def rows(times):
        angles = np.outer(freqs, times)
        return np.concatenate([np.cos(angles), np.sin(angles)], axis=0)

    own = rows(np.arange(ROWS))
    prior = rows(np.arange(-LTAPS, 0))
    tap_order = np.arange(LTAPS).reshape(SEQ, OWN_TAPS).T.reshape(-1)
    taps = rows(tap_order)
    forward = np.concatenate([own, prior, taps], axis=1).astype(ml_dtypes.bfloat16)
    inverse = np.concatenate([own.T, taps.T], axis=0).astype(ml_dtypes.bfloat16)
    return forward, inverse


def lanes(c):
    return pl.ds(pl.multiple_of(c * LANES, LANES), LANES)


def wide(q):
    return pl.ds(pl.multiple_of(q * WIDE, WIDE), WIDE)


def dot(a, b):
    return jnp.dot(a, b, preferred_element_type=F32)


def kernel(
    proj_hbm, og_hbm, sf_hbm, lf_hbm, fw_hbm, iv_hbm,
    gp_hbm, gs_out, gl_out,
    pv, ov, sfv, lfv, fw, iv,
    xs, fs, fkv, gx, gmx, ph, gfh_send, gfh_recv,
    filt_stage, filt, fperm, spec_g, spec_gm, spec_h, y1, y2, y3,
    lperm, gl_send, gl_recv, gl_sum, gs_part, gs_recv, gs_all, gp_v,
    load_sem, store_sem, ph_sem, g_sem, gm_sem, gm0_sem, gf_sem,
    fsend, frecv, lsend, lrecv, ssend, srecv, asend, arecv,
):
    me = lax.axis_index("seq")
    right, left = lax.rem(me + 1, SEQ), lax.rem(me + SEQ - 1, SEQ)
    has_left, has_right = me > 0, me < SEQ - 1

    def peer(i):
        return lax.rem(me + i, SEQ)

    def remote(src, dst, send_sem, recv_sem, to):
        return pltpu.make_async_remote_copy(
            src_ref=src, dst_ref=dst, send_sem=send_sem, recv_sem=recv_sem,
            device_id={"seq": to}, device_id_type=MESH,
        )

    def loop(low, high, body):
        lax.fori_loop(low, high, lambda i, _: (body(i), 0)[1], 0)

    barrier = pltpu.get_barrier_semaphore()
    loop(1, SEQ, lambda i: pl.semaphore_signal(barrier, inc=1, device_id={"seq": peer(i)}, device_id_type=MESH))

    loads = [
        pltpu.make_async_copy(src, dst, load_sem.at[n])
        for n, (src, dst) in enumerate(
            [
                (sf_hbm, sfv), (proj_hbm.at[1], pv.at[1]), (proj_hbm.at[2], pv.at[2]), (proj_hbm.at[0], pv.at[0]),
                (og_hbm, ov), (lf_hbm, lfv), (fw_hbm, fw), (iv_hbm, iv),
            ]
        )
    ]
    for load in loads:
        load.start()

    def feature(s, c, first, count):
        total = None
        for j in range(STAPS):
            term = sfv[s, j : j + 1, lanes(c)] * xs[s, c, pl.ds(EDGE + first - j, count), :]
            total = term if total is None else total + term
        return total

    def gated(c, first, count):
        k, v = feature(1, c, first, count), feature(2, c, first, count)
        fkv[0, c, pl.ds(first, count), :] = k
        fkv[1, c, pl.ds(first, count), :] = v
        gx[pl.ds(LTAPS + first, count), lanes(c)] = (k * v).astype(BF16)

    def mixed(c, first, count):
        cotangent = ov[pl.ds(first, count), lanes(c)].astype(F32)
        gmx[pl.ds(first, count), lanes(c)] = (cotangent * feature(0, c, first, count)).astype(BF16)

    def widen(s, c):
        xs[s, c, pl.ds(EDGE, ROWS), :] = pv[s, :, lanes(c)].astype(F32)

    for load in loads[:3]:
        load.wait()

    def tail(c):
        widen(1, c)
        widen(2, c)
        for first in (128, 192):
            gated(c, first, 64)

    loop(0, CHUNKS, tail)
    loads[3].wait()
    loads[4].wait()

    def head(c):
        widen(0, c)
        for first, count in ((16, 48), (64, 64)):
            mixed(c, first, count)

    loop(0, CHUNKS, head)
    loads[5].wait()
    for q in range(QUADS):
        lperm[0, OWN_TAPS * q : OWN_TAPS * (q + 1), :] = lfv[:, WIDE * q : WIDE * q + LANES]
        lperm[1, OWN_TAPS * q : OWN_TAPS * (q + 1), :] = lfv[:, WIDE * q + LANES : WIDE * (q + 1)]
    filt_stage[:, 0:LANES] = lperm[0, 0:16, :].astype(BF16)
    filt_stage[:, LANES:WIDE] = lperm[1, 0:16, :].astype(BF16)

    pl.semaphore_wait(barrier, SEQ - 1)

    def ph_copy():
        return remote(pv.at[:, pl.ds(ROWS - EDGE, EDGE), :], ph, ph_sem.at[0], ph_sem.at[1], right)

    def g_copy(q):
        return remote(gx.at[pl.ds(ROWS, LTAPS), wide(q)], gx.at[pl.ds(0, LTAPS), wide(q)], g_sem.at[0, q], g_sem.at[1, q], right)

    def gm_copy(q):
        return remote(
            gmx.at[pl.ds(EDGE, LTAPS - EDGE), wide(q)], gmx.at[pl.ds(ROWS + EDGE, LTAPS - EDGE), wide(q)],
            gm_sem.at[0, q], gm_sem.at[1, q], left,
        )

    def gm0_copy():
        return remote(gmx.at[pl.ds(0, EDGE), :], gmx.at[pl.ds(ROWS, EDGE), :], gm0_sem.at[0], gm0_sem.at[1], left)

    def filt_copy(i):
        return remote(filt_stage, filt.at[me], fsend.at[i], frecv.at[me], peer(i))

    def filt_arrival(i):
        return remote(filt_stage, filt.at[peer(i)], fsend.at[i], frecv.at[peer(i)], peer(i))

    @pl.when(has_right)
    def _():
        ph_copy().start()
        loop(0, QUADS, lambda q: g_copy(q).start())

    @pl.when(has_left)
    def _():
        loop(0, QUADS, lambda q: gm_copy(q).start())

    loop(1, SEQ, lambda i: filt_copy(i).start())
    filt[me] = filt_stage[...]

    def rest(c):
        for first, count in ((16, 48), (64, 64)):
            gated(c, first, count)
        for first in (128, 192):
            mixed(c, first, 64)

    loop(0, CHUNKS, rest)

    @pl.when(has_left)
    def _():
        ph_copy().wait_recv()

    @pl.when(jnp.logical_not(has_left))
    def _():
        ph[...] = jnp.zeros_like(ph)
        gx[0:LTAPS, :] = jnp.zeros((LTAPS, COLS), BF16)

    @pl.when(jnp.logical_not(has_right))
    def _():
        gmx[ROWS : ROWS + LTAPS, :] = jnp.zeros((LTAPS, COLS), BF16)
        gfh_recv[...] = jnp.zeros_like(gfh_recv)

    def edge(c):
        for s in range(3):
            xs[s, c, 0:EDGE, :] = ph[s, :, lanes(c)].astype(F32)
        mixed(c, 0, EDGE)
        gated(c, 0, EDGE)

    loop(0, CHUNKS, edge)

    @pl.when(has_left)
    def _():
        gm0_copy().start()

    loads[6].wait()
    loads[7].wait()

    def own_spectra(q):
        spec_g[:, wide(q)] = dot(fw[:, 0:ROWS], gx[LTAPS : LTAPS + ROWS, wide(q)])
        spec_gm[:, wide(q)] = dot(fw[:, 0:ROWS], gmx[0:ROWS, wide(q)])

    loop(0, QUADS, own_spectra)

    loop(1, SEQ, lambda i: filt_arrival(i).wait_recv())

    def unpack(d):
        for half in range(2):
            fperm[half, pl.ds(pl.multiple_of(d * 16, 16), 16), :] = filt[d, :, half * LANES : (half + 1) * LANES].astype(F32)

    loop(0, SEQ, unpack)
    for q in range(QUADS):
        parts = []
        for half in range(2):
            picked = [
                fperm[half, pl.ds(16 * first + OWN_TAPS * q + i, 8, stride=16), :]
                for i in range(OWN_TAPS)
                for first in range(0, SEQ, 8)
            ]
            parts.append(jnp.concatenate(picked, axis=0).astype(BF16))
        taps = jnp.concatenate(parts, axis=1)
        spec_h[:, WIDE * q : WIDE * (q + 1)] = dot(fw[:, ROWS + LTAPS :], taps) * (1.0 / HALF)

    @pl.when(has_right)
    def _():
        gm0_copy().wait_recv()

    def gf_copy(q):
        return remote(gfh_send.at[:, :, wide(q)], gfh_recv.at[:, :, wide(q)], gf_sem.at[0, q], gf_sem.at[1, q], left)

    def s_copy(p):
        return remote(gs_part.at[p], gs_recv.at[me], ssend.at[p], srecv.at[me], p)

    def s_arrival(i):
        return remote(gs_part.at[0], gs_recv.at[peer(i)], ssend.at[0], srecv.at[peer(i)], peer(i))

    def a_copy(i):
        return remote(gs_all.at[me], gs_all.at[me], asend.at[i], arecv.at[me], peer(i))

    def a_arrival(p):
        return remote(gs_all.at[p], gs_all.at[p], asend.at[0], arecv.at[p], p)

    def short_grad(c):
        for s in range(3):
            totals = [None] * STAPS
            for first in range(0, ROWS, 64):
                grad = fs[s, c, pl.ds(first, 64), :]
                for j in range(STAPS):
                    term = jnp.sum((grad * xs[s, c, pl.ds(EDGE + first - j, 64), :]).reshape(8, 8, LANES), axis=0)
                    totals[j] = term if totals[j] is None else totals[j] + term
            rows = [jnp.sum(t, axis=0, keepdims=True) for t in totals] + [jnp.zeros((1, LANES), F32)]
            gs_part[s * CHUNKS + c] = jnp.concatenate(rows, axis=0)

    def main(q):
        @pl.when(has_left)
        def _():
            g_copy(q).wait_recv()

        spec_g[:, wide(q)] += dot(fw[:, ROWS : ROWS + LTAPS], gx[0:LTAPS, wide(q)])

        @pl.when(has_right)
        def _():
            gm_copy(q).wait_recv()

        later = dot(fw[:, ROWS : ROWS + LTAPS], gmx[ROWS : ROWS + LTAPS, wide(q)])
        for first in range(0, HALF, 64):
            re, im = pl.ds(first, 64), pl.ds(HALF + first, 64)
            gc, gi = spec_g[re, wide(q)], spec_g[im, wide(q)]
            oc, oi = spec_gm[re, wide(q)], spec_gm[im, wide(q)]
            hc, hi = spec_h[re, wide(q)], spec_h[im, wide(q)]
            mc, mi = oc - later[first : first + 64], oi - later[HALF + first : HALF + first + 64]
            y1[re, :] = (gc * hc - gi * hi).astype(BF16)
            y1[im, :] = (gc * hi + gi * hc).astype(BF16)
            y2[re, :] = (mc * hc + mi * hi).astype(BF16)
            y2[im, :] = (mi * hc - mc * hi).astype(BF16)
            y3[re, wide(q)] = (oc * gc + oi * gi).astype(BF16)
            y3[im, wide(q)] = (oi * gc - oc * gi).astype(BF16)
        mixing = dot(iv[0:ROWS, :], y1[...])
        grad_gating = dot(iv[0:ROWS, :], y2[...])
        for half in range(2):
            c = 2 * q + half
            part = slice(half * LANES, (half + 1) * LANES)
            fs[0, c, 0:ROWS, :] = ov[:, lanes(c)].astype(F32) * mixing[:, part]
            fs[1, c, 0:ROWS, :] = grad_gating[:, part] * fkv[1, c]
            fs[2, c, 0:ROWS, :] = grad_gating[:, part] * fkv[0, c]
            for s in range(3):
                gfh_send[s, :, lanes(c)] = fs[s, c, 0:EDGE, :].astype(BF16)

        @pl.when(has_left)
        def _():
            gf_copy(q).start()

        for half in range(2):
            short_grad(2 * q + half)
            for s in range(3):
                piece = s * CHUNKS + 2 * q + half

                @pl.when(piece != me)
                def _():
                    s_copy(piece).start()

                @pl.when(piece == me)
                def _():
                    gs_recv[me] = gs_part[piece]

    loop(0, QUADS, main)

    def l_copy(i):
        return remote(gl_send.at[peer(i)], gl_recv.at[me], lsend.at[i], lrecv.at[me], peer(i))

    def l_arrival(i):
        return remote(gl_send.at[peer(i)], gl_recv.at[peer(i)], lsend.at[i], lrecv.at[peer(i)], peer(i))

    for q in range(QUADS):
        partial = dot(iv[ROWS:, :], y3[:, WIDE * q : WIDE * (q + 1)])
        for half in range(2):
            for i in range(OWN_TAPS):
                for first in range(0, SEQ, 8):
                    rows = partial[SEQ * i + first : SEQ * i + first + 8, half * LANES : (half + 1) * LANES]
                    lperm[half, pl.ds(16 * first + OWN_TAPS * q + i, 8, stride=16), :] = rows

    def pack(d):
        for half in range(2):
            gl_send[d, :, half * LANES : (half + 1) * LANES] = lperm[half, pl.ds(pl.multiple_of(d * 16, 16), 16), :].astype(BF16)

    loop(0, SEQ, pack)
    loop(1, SEQ, lambda i: l_copy(i).start())
    gl_recv[me] = gl_send[me]

    @pl.when(me < PIECES)
    def _():
        loop(1, SEQ, lambda i: s_arrival(i).wait_recv())
        total = gs_recv[0]
        for d in range(1, SEQ):
            total = total + gs_recv[d]
        gs_all[me] = total
        loop(1, SEQ, lambda i: a_copy(i).start())

    @pl.when(has_right)
    def _():
        loop(0, QUADS, lambda q: gf_copy(q).wait_recv())

    def gp_store(c):
        return pltpu.make_async_copy(gp_v.at[:, :, lanes(c)], gp_hbm.at[:, :, lanes(c)], store_sem.at[c])

    def back(c):
        for s in range(3):
            fs[s, c, ROWS : ROWS + EDGE, :] = gfh_recv[s, :, lanes(c)].astype(F32)
            for first in range(0, ROWS, 64):
                total = None
                for j in range(STAPS):
                    term = sfv[s, j : j + 1, lanes(c)] * fs[s, c, pl.ds(first + j, 64), :]
                    total = term if total is None else total + term
                gp_v[s, pl.ds(first, 64), lanes(c)] = total.astype(BF16)
        gp_store(c).start()

    loop(0, CHUNKS, back)

    loop(1, SEQ, lambda i: l_arrival(i).wait_recv())
    total = gl_recv[0].astype(F32)
    for d in range(1, SEQ):
        total = total + gl_recv[d].astype(F32)
    gl_sum[...] = total * (1.0 / HALF)
    for q in range(QUADS):
        gl_out[:, WIDE * q : WIDE * (q + 1)] = gl_sum[OWN_TAPS * q : OWN_TAPS * (q + 1), :]

    def a_wait(p):
        @pl.when(p != me)
        def _():
            a_arrival(p).wait_recv()

    loop(0, PIECES, a_wait)
    for s in range(3):
        for c in range(CHUNKS):
            gs_out[s, :, c * LANES : (c + 1) * LANES] = gs_all[s * CHUNKS + c, 0:STAPS, :]

    loop(0, CHUNKS, lambda c: gp_store(c).wait())

    @pl.when(has_right)
    def _():
        ph_copy().wait_send()
        loop(0, QUADS, lambda q: g_copy(q).wait_send())

    @pl.when(has_left)
    def _():
        loop(0, QUADS, lambda q: gm_copy(q).wait_send())
        gm0_copy().wait_send()
        loop(0, QUADS, lambda q: gf_copy(q).wait_send())

    loop(1, SEQ, lambda i: filt_copy(i).wait_send())
    loop(1, SEQ, lambda i: l_copy(i).wait_send())

    def s_sent(p):
        @pl.when(p != me)
        def _():
            s_copy(p).wait_send()

    loop(0, PIECES, s_sent)

    @pl.when(me < PIECES)
    def _():
        loop(1, SEQ, lambda i: a_copy(i).wait_send())


def on_device(projections, out_grad, short_filters, long_filter):
    forward, inverse = transforms()
    dma = pltpu.SemaphoreType.DMA
    vmem = pltpu.VMEM
    scratch = [
        vmem((3, ROWS, COLS), BF16),
        vmem((ROWS, COLS), BF16),
        vmem((3, STAPS, COLS), F32),
        vmem((OWN_TAPS, COLS), F32),
        vmem(forward.shape, BF16),
        vmem(inverse.shape, BF16),
        vmem((3, CHUNKS, EDGE + ROWS, LANES), F32),
        vmem((3, CHUNKS, ROWS + EDGE, LANES), F32),
        vmem((2, CHUNKS, ROWS, LANES), F32),
        vmem((LTAPS + ROWS, COLS), BF16),
        vmem((ROWS + LTAPS, COLS), BF16),
        vmem((3, EDGE, COLS), BF16),
        vmem((3, EDGE, COLS), BF16),
        vmem((3, EDGE, COLS), BF16),
        vmem((16, WIDE), BF16),
        vmem((SEQ, 16, WIDE), BF16),
        vmem((2, SEQ * 16, LANES), F32),
        vmem((POINTS, COLS), F32),
        vmem((POINTS, COLS), F32),
        vmem((POINTS, COLS), F32),
        vmem((POINTS, WIDE), BF16),
        vmem((POINTS, WIDE), BF16),
        vmem((POINTS, COLS), BF16),
        vmem((2, SEQ * 16, LANES), F32),
        vmem((SEQ, 16, WIDE), BF16),
        vmem((SEQ, 16, WIDE), BF16),
        vmem((16, WIDE), F32),
        vmem((PIECES, 8, LANES), F32),
        vmem((SEQ, 8, LANES), F32),
        vmem((PIECES, 8, LANES), F32),
        vmem((3, ROWS, COLS), BF16),
        dma((8,)), dma((CHUNKS,)), dma((2,)), dma((2, QUADS)), dma((2, QUADS)), dma((2,)), dma((2, QUADS)),
        dma((SEQ,)), dma((SEQ,)), dma((SEQ,)), dma((SEQ,)), dma((PIECES,)), dma((SEQ,)), dma((SEQ,)), dma((SEQ,)),
    ]
    hbm = pl.BlockSpec(memory_space=pl.ANY)
    in_vmem = pl.BlockSpec(memory_space=pltpu.VMEM)
    return pl.pallas_call(
        kernel,
        out_shape=(
            jax.ShapeDtypeStruct(projections.shape, BF16),
            jax.ShapeDtypeStruct(short_filters.shape, F32),
            jax.ShapeDtypeStruct(long_filter.shape, F32),
        ),
        in_specs=[hbm] * 6,
        out_specs=(hbm, in_vmem, in_vmem),
        scratch_shapes=scratch,
        compiler_params=pltpu.CompilerParams(collective_id=0, has_side_effects=True, vmem_limit_bytes=50 << 20),
    )(projections, out_grad, short_filters, long_filter, jnp.asarray(forward), jnp.asarray(inverse))


def solution(mesh):
    in_specs = (
        P(None, "seq", "tensor"),
        P("seq", "tensor"),
        P(None, None, "tensor"),
        P("seq", "tensor"),
    )
    out_specs = (P(None, "seq", "tensor"), P(None, None, "tensor"), P("seq", "tensor"))
    return jax.shard_map(on_device, mesh=mesh, in_specs=in_specs, out_specs=out_specs, check_vma=False)
```

```python
import jax
import jax.numpy as jnp
import ml_dtypes
import numpy as np
from jax import lax
from jax.experimental import pallas as pl
from jax.experimental.pallas import tpu as pltpu
from jax.sharding import PartitionSpec as P

MESH = pl.DeviceIdType.MESH
F32 = jnp.float32
BF16 = jnp.bfloat16

STAPS = 7
LTAPS = 128
ROWS = 256
COLS = 1024
LANES = 128
CHUNKS = COLS // LANES
WIDE = 256
QUADS = COLS // WIDE
SEQ = 32
OWN_TAPS = LTAPS // SEQ
POINTS = ROWS + LTAPS
HALF = POINTS // 2
EDGE = 16
PIECES = 3 * CHUNKS
ROW = 4
COLUMN = 8
FIRST_OWNER = 12
HALO = STAPS - 1


def transforms():
    freqs = 2.0 * np.pi * (np.arange(HALF) + 0.5) / POINTS

    def rows(times):
        angles = np.outer(freqs, times)
        return np.concatenate([np.cos(angles), np.sin(angles)], axis=0)

    own = rows(np.arange(ROWS))
    prior = rows(np.arange(-LTAPS, 0))
    tap_order = np.arange(LTAPS).reshape(SEQ, OWN_TAPS).T.reshape(-1)
    taps = rows(tap_order)
    forward = np.concatenate([own, prior, taps], axis=1).astype(ml_dtypes.bfloat16)
    inverse = np.concatenate([own.T, taps.T], axis=0).astype(ml_dtypes.bfloat16)
    return forward, inverse


def lanes(c):
    return pl.ds(pl.multiple_of(c * LANES, LANES), LANES)


def wide(q):
    return pl.ds(pl.multiple_of(q * WIDE, WIDE), WIDE)


def dot(a, b):
    return jnp.dot(a, b, preferred_element_type=F32)


def kernel(
    proj_hbm, og_hbm, sf_hbm, lf_hbm, fw_hbm, iv_hbm,
    gp_hbm, gs_out, gl_out,
    pv, ov, sfv, lfv, fw, iv,
    xs, fs, fkv, gx, gmx, ph_stage, ph_send, ph_recv, gf_stage, gf_send, gf_recv,
    filt_a, filt_b, fperm, spec_g, spec_gm, spec_h, y1, y2,
    lperm, gl_send, gl_recv, gl_sum, gs_part, gs_recv, gs_all, gp_v,
    load_sem, store_sem, ph_sem, g_sem, gm_sem, gm0_sem, gf_sem,
    fsend, frecv, lsend, lrecv, ssend, srecv, asend, arecv,
):
    me = lax.axis_index("seq")
    right, left = lax.rem(me + 1, SEQ), lax.rem(me + SEQ - 1, SEQ)
    has_left, has_right = me > 0, me < SEQ - 1

    def peer(i):
        return lax.rem(me + i, SEQ)

    def remote(src, dst, send_sem, recv_sem, to):
        return pltpu.make_async_remote_copy(
            src_ref=src, dst_ref=dst, send_sem=send_sem, recv_sem=recv_sem,
            device_id={"seq": to}, device_id_type=MESH,
        )

    def loop(low, high, body):
        lax.fori_loop(low, high, lambda i, _: (body(i), 0)[1], 0)

    y, z = lax.rem(me, ROW), lax.div(me, ROW)

    def in_row(i):
        return z * ROW + lax.rem(y + i, ROW)

    def in_column(i):
        return lax.rem(z + i, COLUMN) * ROW + y

    barrier = pltpu.get_barrier_semaphore()
    greeted = [left, right] + [in_row(i) for i in range(1, ROW)] + [in_column(i) for i in range(1, COLUMN)]
    for other in greeted:
        pl.semaphore_signal(barrier, inc=1, device_id={"seq": other}, device_id_type=MESH)

    loads = [
        pltpu.make_async_copy(src, dst, load_sem.at[n])
        for n, (src, dst) in enumerate(
            [
                (sf_hbm, sfv), (proj_hbm.at[1], pv.at[1]), (proj_hbm.at[2], pv.at[2]), (proj_hbm.at[0], pv.at[0]),
                (og_hbm, ov), (lf_hbm, lfv), (fw_hbm, fw), (iv_hbm, iv),
            ]
        )
    ]
    for load in loads:
        load.start()

    def feature(s, c, first, count):
        total = None
        for j in range(STAPS):
            term = sfv[s, j : j + 1, lanes(c)] * xs[s, c, pl.ds(EDGE + first - j, count), :]
            total = term if total is None else total + term
        return total

    def gated(c, first, count):
        k, v = feature(1, c, first, count), feature(2, c, first, count)
        fkv[0, c, pl.ds(first, count), :] = k
        fkv[1, c, pl.ds(first, count), :] = v
        gx[pl.ds(LTAPS + first, count), lanes(c)] = (k * v).astype(BF16)

    def mixed(c, first, count):
        cotangent = ov[pl.ds(first, count), lanes(c)].astype(F32)
        gmx[pl.ds(first, count), lanes(c)] = (cotangent * feature(0, c, first, count)).astype(BF16)

    def widen(s, c):
        xs[s, c, pl.ds(EDGE, ROWS), :] = pv[s, :, lanes(c)].astype(F32)

    for load in loads[:3]:
        load.wait()

    def tail(c):
        widen(1, c)
        widen(2, c)
        for first in (128, 192):
            gated(c, first, 64)

    loop(0, CHUNKS, tail)
    loads[3].wait()
    loads[4].wait()

    def head(c):
        widen(0, c)
        for first, count in ((16, 48), (64, 64)):
            mixed(c, first, count)

    loop(0, CHUNKS, head)
    loads[5].wait()
    for q in range(QUADS):
        lperm[0, OWN_TAPS * q : OWN_TAPS * (q + 1), :] = lfv[:, WIDE * q : WIDE * q + LANES]
        lperm[1, OWN_TAPS * q : OWN_TAPS * (q + 1), :] = lfv[:, WIDE * q + LANES : WIDE * (q + 1)]
    filt_a[z, y] = lperm[0, 0:16, :].astype(BF16)
    filt_b[y, z] = lperm[1, 0:16, :].astype(BF16)

    def fold(stage, source, first, packed):
        for c in range(CHUNKS):
            stage[c, 0:6, :] = source[0, c, first : first + 6, :]
            stage[c, 6:12, :] = source[1, c, first : first + 6, :]
            stage[c, 12:16, :] = source[2, c, first : first + 4, :]
            stage[CHUNKS, 2 * c : 2 * c + 2, :] = source[2, c, first + 4 : first + 6, :]
        for c in range(CHUNKS + 1):
            packed[:, LANES * c : LANES * (c + 1)] = stage[c].astype(BF16)

    def unfold(packed, stage, target, first):
        for c in range(CHUNKS + 1):
            stage[c] = packed[:, LANES * c : LANES * (c + 1)].astype(F32)
        for c in range(CHUNKS):
            target[0, c, first : first + 6, :] = stage[c, 0:6, :]
            target[1, c, first : first + 6, :] = stage[c, 6:12, :]
            target[2, c, first : first + 4, :] = stage[c, 12:16, :]
            target[2, c, first + 4 : first + 6, :] = stage[CHUNKS, 2 * c : 2 * c + 2, :]

    fold(ph_stage, xs, EDGE + ROWS - HALO, ph_send)

    pl.semaphore_wait(barrier, len(greeted))

    def ph_copy():
        return remote(ph_send, ph_recv, ph_sem.at[0], ph_sem.at[1], right)

    def g_copy(q):
        return remote(gx.at[pl.ds(ROWS, LTAPS), wide(q)], gx.at[pl.ds(0, LTAPS), wide(q)], g_sem.at[0, q], g_sem.at[1, q], right)

    def gm_copy(q):
        return remote(
            gmx.at[pl.ds(EDGE, LTAPS - EDGE), wide(q)], gmx.at[pl.ds(ROWS + EDGE, LTAPS - EDGE), wide(q)],
            gm_sem.at[0, q], gm_sem.at[1, q], left,
        )

    def gm0_copy():
        return remote(gmx.at[pl.ds(0, EDGE), :], gmx.at[pl.ds(ROWS, EDGE), :], gm0_sem.at[0], gm0_sem.at[1], left)

    def a1_copy(i):
        return remote(filt_a.at[z, y], filt_a.at[z, y], fsend.at[i], frecv.at[i], in_row(i))

    def a2_copy(i):
        return remote(filt_a.at[z], filt_a.at[z], fsend.at[ROW + i], frecv.at[ROW + i], in_column(i))

    def b1_copy(i):
        return remote(filt_b.at[y, z], filt_b.at[y, z], fsend.at[12 + i], frecv.at[12 + i], in_column(i))

    def b2_copy(i):
        return remote(filt_b.at[y], filt_b.at[y], fsend.at[20 + i], frecv.at[20 + i], in_row(i))

    loop(1, ROW, lambda i: a1_copy(i).start())
    loop(1, COLUMN, lambda i: b1_copy(i).start())

    @pl.when(has_right)
    def _():
        ph_copy().start()
        loop(0, QUADS, lambda q: g_copy(q).start())

    @pl.when(has_left)
    def _():
        loop(0, QUADS, lambda q: gm_copy(q).start())

    def rest(c):
        for first, count in ((16, 48), (64, 64)):
            gated(c, first, count)
        for first in (128, 192):
            mixed(c, first, 64)

    loop(0, CHUNKS, rest)

    @pl.when(has_left)
    def _():
        ph_copy().wait_recv()

    @pl.when(jnp.logical_not(has_left))
    def _():
        ph_recv[...] = jnp.zeros_like(ph_recv)
        gx[0:LTAPS, :] = jnp.zeros((LTAPS, COLS), BF16)

    @pl.when(jnp.logical_not(has_right))
    def _():
        gmx[ROWS : ROWS + LTAPS, :] = jnp.zeros((LTAPS, COLS), BF16)
        gf_recv[...] = jnp.zeros_like(gf_recv)

    unfold(ph_recv, ph_stage, xs, EDGE - HALO)

    def edge(c):
        mixed(c, 0, EDGE)
        gated(c, 0, EDGE)

    loop(0, CHUNKS, edge)

    @pl.when(has_left)
    def _():
        gm0_copy().start()

    loop(1, ROW, lambda i: a1_copy(i).wait_recv())
    loop(1, COLUMN, lambda i: a2_copy(i).start())

    loads[6].wait()
    loads[7].wait()

    def own_spectra(q):
        spec_g[:, wide(q)] = dot(fw[:, 0:ROWS], gx[LTAPS : LTAPS + ROWS, wide(q)])
        spec_gm[:, wide(q)] = dot(fw[:, 0:ROWS], gmx[0:ROWS, wide(q)])

    loop(0, QUADS, own_spectra)

    loop(1, COLUMN, lambda i: b1_copy(i).wait_recv())
    loop(1, ROW, lambda i: b2_copy(i).start())

    for q in range(QUADS):

        @pl.when(has_left)
        def _():
            g_copy(q).wait_recv()

        spec_g[:, WIDE * q : WIDE * (q + 1)] += dot(fw[:, ROWS : ROWS + LTAPS], gx[0:LTAPS, WIDE * q : WIDE * (q + 1)])
        for first in range(0, HALF, 64):
            re, im = pl.ds(first, 64), pl.ds(HALF + first, 64)
            cols = pl.ds(WIDE * q, WIDE)
            gc, gi = spec_g[re, cols], spec_g[im, cols]
            oc, oi = spec_gm[re, cols], spec_gm[im, cols]
            y1[re, :] = (oc * gc + oi * gi).astype(BF16)
            y1[im, :] = (oi * gc - oc * gi).astype(BF16)
        partial = dot(iv[ROWS:, :], y1[...])
        for half in range(2):
            for i in range(OWN_TAPS):
                for first in range(0, SEQ, 8):
                    rows = partial[SEQ * i + first : SEQ * i + first + 8, half * LANES : (half + 1) * LANES]
                    lperm[half, pl.ds(16 * first + OWN_TAPS * q + i, 8, stride=16), :] = rows

    def pack(d):
        for half in range(2):
            gl_send[d, :, half * LANES : (half + 1) * LANES] = lperm[half, pl.ds(pl.multiple_of(d * 16, 16), 16), :].astype(BF16)

    loop(0, SEQ, pack)

    loop(1, COLUMN, lambda i: a2_copy(i).wait_recv())
    loop(1, ROW, lambda i: b2_copy(i).wait_recv())

    def l_copy(i):
        return remote(gl_send.at[peer(i)], gl_recv.at[me], lsend.at[i], lrecv.at[me], peer(i))

    def l_arrival(i):
        return remote(gl_send.at[peer(i)], gl_recv.at[peer(i)], lsend.at[i], lrecv.at[peer(i)], peer(i))

    loop(1, SEQ, lambda i: l_copy(i).start())
    gl_recv[me] = gl_send[me]

    def unpack(d):
        rows = pl.ds(pl.multiple_of(d * 16, 16), 16)
        dz, dy = lax.div(d, ROW), lax.rem(d, ROW)
        fperm[0, rows, :] = filt_a[dz, dy].astype(F32)
        fperm[1, rows, :] = filt_b[dy, dz].astype(F32)

    loop(0, SEQ, unpack)
    for q in range(QUADS):
        parts = []
        for half in range(2):
            picked = [
                fperm[half, pl.ds(16 * first + OWN_TAPS * q + i, 8, stride=16), :]
                for i in range(OWN_TAPS)
                for first in range(0, SEQ, 8)
            ]
            parts.append(jnp.concatenate(picked, axis=0).astype(BF16))
        taps = jnp.concatenate(parts, axis=1)
        spec_h[:, WIDE * q : WIDE * (q + 1)] = dot(fw[:, ROWS + LTAPS :], taps) * (1.0 / HALF)

    @pl.when(has_right)
    def _():
        gm0_copy().wait_recv()

    def gf_copy():
        return remote(gf_send, gf_recv, gf_sem.at[0], gf_sem.at[1], left)

    my_piece = lax.rem(me + SEQ - FIRST_OWNER, SEQ)

    def owner(p):
        return lax.rem(p + FIRST_OWNER, SEQ)

    def s_copy(p):
        return remote(gs_part.at[p], gs_recv.at[me], ssend.at[p], srecv.at[me], owner(p))

    def s_arrival(i):
        return remote(gs_part.at[0], gs_recv.at[peer(i)], ssend.at[0], srecv.at[peer(i)], peer(i))

    def a_copy(d):
        return remote(gs_all.at[my_piece], gs_all.at[my_piece], asend.at[d], arecv.at[my_piece], d)

    def a_arrival(p):
        return remote(gs_all.at[p], gs_all.at[p], asend.at[0], arecv.at[p], owner(p))

    def short_grad(c):
        for s in range(3):
            totals = [None] * STAPS
            for first in range(0, ROWS, 64):
                grad = fs[s, c, pl.ds(first, 64), :]
                for j in range(STAPS):
                    term = jnp.sum((grad * xs[s, c, pl.ds(EDGE + first - j, 64), :]).reshape(8, 8, LANES), axis=0)
                    totals[j] = term if totals[j] is None else totals[j] + term
            rows = [jnp.sum(t, axis=0, keepdims=True) for t in totals] + [jnp.zeros((1, LANES), F32)]
            gs_part[3 * c + s] = jnp.concatenate(rows, axis=0)

    def main(q):
        @pl.when(has_right)
        def _():
            gm_copy(q).wait_recv()

        later = dot(fw[:, ROWS : ROWS + LTAPS], gmx[ROWS : ROWS + LTAPS, wide(q)])
        for first in range(0, HALF, 64):
            re, im = pl.ds(first, 64), pl.ds(HALF + first, 64)
            gc, gi = spec_g[re, wide(q)], spec_g[im, wide(q)]
            oc, oi = spec_gm[re, wide(q)], spec_gm[im, wide(q)]
            hc, hi = spec_h[re, wide(q)], spec_h[im, wide(q)]
            mc, mi = oc - later[first : first + 64], oi - later[HALF + first : HALF + first + 64]
            y1[re, :] = (gc * hc - gi * hi).astype(BF16)
            y1[im, :] = (gc * hi + gi * hc).astype(BF16)
            y2[re, :] = (mc * hc + mi * hi).astype(BF16)
            y2[im, :] = (mi * hc - mc * hi).astype(BF16)
        mixing = dot(iv[0:ROWS, :], y1[...])
        grad_gating = dot(iv[0:ROWS, :], y2[...])
        for half in range(2):
            c = 2 * q + half
            part = slice(half * LANES, (half + 1) * LANES)
            fs[0, c, 0:ROWS, :] = ov[:, lanes(c)].astype(F32) * mixing[:, part]
            fs[1, c, 0:ROWS, :] = grad_gating[:, part] * fkv[1, c]
            fs[2, c, 0:ROWS, :] = grad_gating[:, part] * fkv[0, c]

        for half in range(2):
            short_grad(2 * q + half)
            for s in range(3):
                piece = 3 * (2 * q + half) + s

                @pl.when(piece != my_piece)
                def _():
                    s_copy(piece).start()

                @pl.when(piece == my_piece)
                def _():
                    gs_recv[me] = gs_part[piece]

    loop(0, QUADS, main)

    fold(gf_stage, fs, 0, gf_send)

    @pl.when(has_left)
    def _():
        gf_copy().start()

    def back(c, first, count):
        for s in range(3):
            total = None
            for j in range(STAPS):
                term = sfv[s, j : j + 1, lanes(c)] * fs[s, c, pl.ds(first + j, count), :]
                total = term if total is None else total + term
            gp_v[s, pl.ds(first, count), lanes(c)] = total.astype(BF16)

    def back_bulk(c):
        for first, count in ((0, 64), (64, 64), (128, 64), (192, 48)):
            back(c, first, count)

    loop(0, CHUNKS, back_bulk)

    def gp_store(c):
        return pltpu.make_async_copy(gp_v.at[:, :, lanes(c)], gp_hbm.at[:, :, lanes(c)], store_sem.at[c])

    @pl.when(has_right)
    def _():
        gf_copy().wait_recv()

    unfold(gf_recv, gf_stage, fs, ROWS)

    def back_edge(c):
        back(c, ROWS - EDGE, EDGE)
        gp_store(c).start()

    loop(0, CHUNKS, back_edge)

    def hand_out(d):
        @pl.when(d != me)
        def _():
            a_copy(d).start()

    @pl.when(my_piece < PIECES)
    def _():
        loop(1, SEQ, lambda i: s_arrival(i).wait_recv())
        total = gs_recv[0]
        for d in range(1, SEQ):
            total = total + gs_recv[d]
        gs_all[my_piece] = total
        loop(0, SEQ, hand_out)

    loop(1, SEQ, lambda i: l_arrival(i).wait_recv())
    total = gl_recv[0].astype(F32)
    for d in range(1, SEQ):
        total = total + gl_recv[d].astype(F32)
    gl_sum[...] = total * (1.0 / HALF)
    for q in range(QUADS):
        gl_out[:, WIDE * q : WIDE * (q + 1)] = gl_sum[OWN_TAPS * q : OWN_TAPS * (q + 1), :]

    @pl.when(has_right)
    def _():
        ph_copy().wait_send()
        loop(0, QUADS, lambda q: g_copy(q).wait_send())

    @pl.when(has_left)
    def _():
        loop(0, QUADS, lambda q: gm_copy(q).wait_send())
        gm0_copy().wait_send()
        gf_copy().wait_send()

    for i in range(1, ROW):
        a1_copy(i).wait_send()
        b2_copy(i).wait_send()
    for i in range(1, COLUMN):
        a2_copy(i).wait_send()
        b1_copy(i).wait_send()
    loop(1, SEQ, lambda i: l_copy(i).wait_send())

    def s_sent(p):
        @pl.when(p != my_piece)
        def _():
            s_copy(p).wait_send()

    loop(0, PIECES, s_sent)

    def a_sent(d):
        @pl.when(d != me)
        def _():
            a_copy(d).wait_send()

    @pl.when(my_piece < PIECES)
    def _():
        loop(0, SEQ, a_sent)

    loop(0, CHUNKS, lambda c: gp_store(c).wait())

    def a_wait(p):
        @pl.when(p != my_piece)
        def _():
            a_arrival(p).wait_recv()

    loop(0, PIECES, a_wait)
    for s in range(3):
        for c in range(CHUNKS):
            gs_out[s, :, c * LANES : (c + 1) * LANES] = gs_all[3 * c + s, 0:STAPS, :]


def on_device(projections, out_grad, short_filters, long_filter):
    forward, inverse = transforms()
    dma = pltpu.SemaphoreType.DMA
    vmem = pltpu.VMEM
    scratch = [
        vmem((3, ROWS, COLS), BF16),
        vmem((ROWS, COLS), BF16),
        vmem((3, STAPS, COLS), F32),
        vmem((OWN_TAPS, COLS), F32),
        vmem(forward.shape, BF16),
        vmem(inverse.shape, BF16),
        vmem((3, CHUNKS, EDGE + ROWS, LANES), F32),
        vmem((3, CHUNKS, ROWS + EDGE, LANES), F32),
        vmem((2, CHUNKS, ROWS, LANES), F32),
        vmem((LTAPS + ROWS, COLS), BF16),
        vmem((ROWS + LTAPS, COLS), BF16),
        vmem((CHUNKS + 1, EDGE, LANES), F32),
        vmem((EDGE, COLS + LANES), BF16),
        vmem((EDGE, COLS + LANES), BF16),
        vmem((CHUNKS + 1, EDGE, LANES), F32),
        vmem((EDGE, COLS + LANES), BF16),
        vmem((EDGE, COLS + LANES), BF16),
        vmem((COLUMN, ROW, 16, LANES), BF16),
        vmem((ROW, COLUMN, 16, LANES), BF16),
        vmem((2, SEQ * 16, LANES), F32),
        vmem((POINTS, COLS), F32),
        vmem((POINTS, COLS), F32),
        vmem((POINTS, COLS), F32),
        vmem((POINTS, WIDE), BF16),
        vmem((POINTS, WIDE), BF16),
        vmem((2, SEQ * 16, LANES), F32),
        vmem((SEQ, 16, WIDE), BF16),
        vmem((SEQ, 16, WIDE), BF16),
        vmem((16, WIDE), F32),
        vmem((PIECES, 8, LANES), F32),
        vmem((SEQ, 8, LANES), F32),
        vmem((PIECES, 8, LANES), F32),
        vmem((3, ROWS, COLS), BF16),
        dma((8,)), dma((CHUNKS,)), dma((2,)), dma((2, QUADS)), dma((2, QUADS)), dma((2,)), dma((2,)),
        dma((SEQ,)), dma((SEQ,)), dma((SEQ,)), dma((SEQ,)), dma((PIECES,)), dma((SEQ,)), dma((SEQ,)), dma((SEQ,)),
    ]
    hbm = pl.BlockSpec(memory_space=pltpu.HBM)
    in_vmem = pl.BlockSpec(memory_space=pltpu.VMEM)
    return pl.pallas_call(
        kernel,
        out_shape=(
            jax.ShapeDtypeStruct(projections.shape, BF16),
            jax.ShapeDtypeStruct(short_filters.shape, F32),
            jax.ShapeDtypeStruct(long_filter.shape, F32),
        ),
        in_specs=[hbm] * 6,
        out_specs=(hbm, in_vmem, in_vmem),
        scratch_shapes=scratch,
        compiler_params=pltpu.CompilerParams(collective_id=0, has_side_effects=True, vmem_limit_bytes=50 << 20),
    )(projections, out_grad, short_filters, long_filter, jnp.asarray(forward), jnp.asarray(inverse))


def solution(mesh):
    in_specs = (
        P(None, "seq", "tensor"),
        P("seq", "tensor"),
        P(None, None, "tensor"),
        P("seq", "tensor"),
    )
    out_specs = (P(None, "seq", "tensor"), P(None, None, "tensor"), P("seq", "tensor"))
    return jax.shard_map(on_device, mesh=mesh, in_specs=in_specs, out_specs=out_specs, check_vma=False)
```

```python
import jax
import jax.numpy as jnp
import ml_dtypes
import numpy as np
from jax import lax
from jax.experimental import pallas as pl
from jax.experimental.pallas import tpu as pltpu
from jax.sharding import PartitionSpec as P

MESH = pl.DeviceIdType.MESH
F32 = jnp.float32
BF16 = jnp.bfloat16

STAPS = 7
LTAPS = 128
ROWS = 256
COLS = 1024
LANES = 128
CHUNKS = COLS // LANES
WIDE = 256
QUADS = COLS // WIDE
SEQ = 32
OWN_TAPS = LTAPS // SEQ
POINTS = ROWS + LTAPS
HALF = POINTS // 2
EDGE = 16
PIECES = 3 * CHUNKS
ROW = 4
COLUMN = 8
FIRST_OWNER = 12
HALO = STAPS - 1


def transforms():
    freqs = 2.0 * np.pi * (np.arange(HALF) + 0.5) / POINTS

    def rows(times):
        angles = np.outer(freqs, times)
        return np.concatenate([np.cos(angles), np.sin(angles)], axis=0)

    own = rows(np.arange(ROWS))
    prior = rows(np.arange(-LTAPS, 0))
    tap_order = np.arange(LTAPS).reshape(SEQ, OWN_TAPS).T.reshape(-1)
    taps = rows(tap_order)
    forward = np.concatenate([own, prior, taps], axis=1).astype(ml_dtypes.bfloat16)
    inverse = np.concatenate([own.T, taps.T], axis=0).astype(ml_dtypes.bfloat16)
    return forward, inverse


def lanes(c):
    return pl.ds(pl.multiple_of(c * LANES, LANES), LANES)


def wide(q):
    return pl.ds(pl.multiple_of(q * WIDE, WIDE), WIDE)


def dot(a, b):
    return jnp.dot(a, b, preferred_element_type=F32)


def kernel(
    proj_hbm, og_hbm, sf_hbm, lf_hbm, fw_hbm, iv_hbm,
    gp_v, gs_out, gl_out,
    pv, ov, sfv, lfv, fw, iv,
    xs, fs, fkv, gx, gmx, ph_stage, ph_send, ph_recv, gf_stage, gf_send, gf_recv,
    filt_a, filt_b, fperm, spec_g, spec_gm, spec_h, y1, y2,
    lperm, gl_send, gl_recv, gl_sum, gs_part, gs_recv, gs_all,
    load_sem, ph_sem, g_sem, gm_sem, gm0_sem, gf_sem,
    fsend, frecv, lsend, lrecv, ssend, srecv, asend, arecv,
):
    me = lax.axis_index("seq")
    right, left = lax.rem(me + 1, SEQ), lax.rem(me + SEQ - 1, SEQ)
    has_left, has_right = me > 0, me < SEQ - 1

    def peer(i):
        return lax.rem(me + i, SEQ)

    def remote(src, dst, send_sem, recv_sem, to):
        return pltpu.make_async_remote_copy(
            src_ref=src, dst_ref=dst, send_sem=send_sem, recv_sem=recv_sem,
            device_id={"seq": to}, device_id_type=MESH,
        )

    def loop(low, high, body):
        lax.fori_loop(low, high, lambda i, _: (body(i), 0)[1], 0)

    y, z = lax.rem(me, ROW), lax.div(me, ROW)

    def in_row(i):
        return z * ROW + lax.rem(y + i, ROW)

    def in_column(i):
        return lax.rem(z + i, COLUMN) * ROW + y

    barrier = pltpu.get_barrier_semaphore()
    greeted = [left, right] + [in_row(i) for i in range(1, ROW)] + [in_column(i) for i in range(1, COLUMN)]
    for other in greeted:
        pl.semaphore_signal(barrier, inc=1, device_id={"seq": other}, device_id_type=MESH)

    loads = [
        pltpu.make_async_copy(src, dst, load_sem.at[n])
        for n, (src, dst) in enumerate(
            [
                (sf_hbm, sfv), (proj_hbm.at[1], pv.at[1]), (proj_hbm.at[2], pv.at[2]), (proj_hbm.at[0], pv.at[0]),
                (og_hbm, ov), (lf_hbm, lfv), (fw_hbm, fw), (iv_hbm, iv),
            ]
        )
    ]
    for load in loads:
        load.start()

    def feature(s, c, first, count):
        total = None
        for j in range(STAPS):
            term = sfv[s, j : j + 1, lanes(c)] * xs[s, c, pl.ds(EDGE + first - j, count), :]
            total = term if total is None else total + term
        return total

    def gated(c, first, count):
        k, v = feature(1, c, first, count), feature(2, c, first, count)
        fkv[0, c, pl.ds(first, count), :] = k
        fkv[1, c, pl.ds(first, count), :] = v
        gx[pl.ds(LTAPS + first, count), lanes(c)] = (k * v).astype(BF16)

    def mixed(c, first, count):
        cotangent = ov[pl.ds(first, count), lanes(c)].astype(F32)
        gmx[pl.ds(first, count), lanes(c)] = (cotangent * feature(0, c, first, count)).astype(BF16)

    def widen(s, c):
        xs[s, c, pl.ds(EDGE, ROWS), :] = pv[s, :, lanes(c)].astype(F32)

    for load in loads[:3]:
        load.wait()

    def tail(c):
        widen(1, c)
        widen(2, c)
        for first in (128, 192):
            gated(c, first, 64)

    loop(0, CHUNKS, tail)
    loads[3].wait()
    loads[4].wait()

    def head(c):
        widen(0, c)
        for first, count in ((16, 48), (64, 64)):
            mixed(c, first, count)

    loop(0, CHUNKS, head)
    loads[5].wait()
    for q in range(QUADS):
        lperm[0, OWN_TAPS * q : OWN_TAPS * (q + 1), :] = lfv[:, WIDE * q : WIDE * q + LANES]
        lperm[1, OWN_TAPS * q : OWN_TAPS * (q + 1), :] = lfv[:, WIDE * q + LANES : WIDE * (q + 1)]
    filt_a[z, y] = lperm[0, 0:16, :].astype(BF16)
    filt_b[y, z] = lperm[1, 0:16, :].astype(BF16)

    def fold(stage, source, first, packed):
        for c in range(CHUNKS):
            stage[c, 0:6, :] = source[0, c, first : first + 6, :]
            stage[c, 6:12, :] = source[1, c, first : first + 6, :]
            stage[c, 12:16, :] = source[2, c, first : first + 4, :]
            stage[CHUNKS, 2 * c : 2 * c + 2, :] = source[2, c, first + 4 : first + 6, :]
        for c in range(CHUNKS + 1):
            packed[:, LANES * c : LANES * (c + 1)] = stage[c].astype(BF16)

    def unfold(packed, stage, target, first):
        for c in range(CHUNKS + 1):
            stage[c] = packed[:, LANES * c : LANES * (c + 1)].astype(F32)
        for c in range(CHUNKS):
            target[0, c, first : first + 6, :] = stage[c, 0:6, :]
            target[1, c, first : first + 6, :] = stage[c, 6:12, :]
            target[2, c, first : first + 4, :] = stage[c, 12:16, :]
            target[2, c, first + 4 : first + 6, :] = stage[CHUNKS, 2 * c : 2 * c + 2, :]

    fold(ph_stage, xs, EDGE + ROWS - HALO, ph_send)

    pl.semaphore_wait(barrier, len(greeted))

    def ph_copy():
        return remote(ph_send, ph_recv, ph_sem.at[0], ph_sem.at[1], right)

    def g_copy(q):
        return remote(gx.at[pl.ds(ROWS, LTAPS), wide(q)], gx.at[pl.ds(0, LTAPS), wide(q)], g_sem.at[0, q], g_sem.at[1, q], right)

    def gm_copy(q):
        return remote(
            gmx.at[pl.ds(EDGE, LTAPS - EDGE), wide(q)], gmx.at[pl.ds(ROWS + EDGE, LTAPS - EDGE), wide(q)],
            gm_sem.at[0, q], gm_sem.at[1, q], left,
        )

    def gm0_copy():
        return remote(gmx.at[pl.ds(0, EDGE), :], gmx.at[pl.ds(ROWS, EDGE), :], gm0_sem.at[0], gm0_sem.at[1], left)

    def a1_copy(i):
        return remote(filt_a.at[z, y], filt_a.at[z, y], fsend.at[i], frecv.at[i], in_row(i))

    def a2_copy(i):
        return remote(filt_a.at[z], filt_a.at[z], fsend.at[ROW + i], frecv.at[ROW + i], in_column(i))

    def b1_copy(i):
        return remote(filt_b.at[y, z], filt_b.at[y, z], fsend.at[12 + i], frecv.at[12 + i], in_column(i))

    def b2_copy(i):
        return remote(filt_b.at[y], filt_b.at[y], fsend.at[20 + i], frecv.at[20 + i], in_row(i))

    loop(1, ROW, lambda i: a1_copy(i).start())
    loop(1, COLUMN, lambda i: b1_copy(i).start())

    @pl.when(has_right)
    def _():
        ph_copy().start()
        loop(0, QUADS, lambda q: g_copy(q).start())

    @pl.when(has_left)
    def _():
        loop(0, QUADS, lambda q: gm_copy(q).start())

    def rest(c):
        for first, count in ((16, 48), (64, 64)):
            gated(c, first, count)
        for first in (128, 192):
            mixed(c, first, 64)

    loop(0, CHUNKS, rest)

    @pl.when(has_left)
    def _():
        ph_copy().wait_recv()

    @pl.when(jnp.logical_not(has_left))
    def _():
        ph_recv[...] = jnp.zeros_like(ph_recv)
        gx[0:LTAPS, :] = jnp.zeros((LTAPS, COLS), BF16)

    @pl.when(jnp.logical_not(has_right))
    def _():
        gmx[ROWS : ROWS + LTAPS, :] = jnp.zeros((LTAPS, COLS), BF16)
        gf_recv[...] = jnp.zeros_like(gf_recv)

    unfold(ph_recv, ph_stage, xs, EDGE - HALO)

    def edge(c):
        mixed(c, 0, EDGE)
        gated(c, 0, EDGE)

    loop(0, CHUNKS, edge)

    @pl.when(has_left)
    def _():
        gm0_copy().start()

    loop(1, ROW, lambda i: a1_copy(i).wait_recv())
    loop(1, COLUMN, lambda i: a2_copy(i).start())

    loads[6].wait()
    loads[7].wait()

    def own_spectra(q):
        spec_g[:, wide(q)] = dot(fw[:, 0:ROWS], gx[LTAPS : LTAPS + ROWS, wide(q)])
        spec_gm[:, wide(q)] = dot(fw[:, 0:ROWS], gmx[0:ROWS, wide(q)])

    loop(0, QUADS, own_spectra)

    loop(1, COLUMN, lambda i: b1_copy(i).wait_recv())
    loop(1, ROW, lambda i: b2_copy(i).start())

    for q in range(QUADS):

        @pl.when(has_left)
        def _():
            g_copy(q).wait_recv()

        spec_g[:, WIDE * q : WIDE * (q + 1)] += dot(fw[:, ROWS : ROWS + LTAPS], gx[0:LTAPS, WIDE * q : WIDE * (q + 1)])
        for first in range(0, HALF, 64):
            re, im = pl.ds(first, 64), pl.ds(HALF + first, 64)
            cols = pl.ds(WIDE * q, WIDE)
            gc, gi = spec_g[re, cols], spec_g[im, cols]
            oc, oi = spec_gm[re, cols], spec_gm[im, cols]
            y1[re, :] = (oc * gc + oi * gi).astype(BF16)
            y1[im, :] = (oi * gc - oc * gi).astype(BF16)
        partial = dot(iv[ROWS:, :], y1[...])
        for half in range(2):
            for i in range(OWN_TAPS):
                for first in range(0, SEQ, 8):
                    rows = partial[SEQ * i + first : SEQ * i + first + 8, half * LANES : (half + 1) * LANES]
                    lperm[half, pl.ds(16 * first + OWN_TAPS * q + i, 8, stride=16), :] = rows

    def pack(d):
        for half in range(2):
            gl_send[d, :, half * LANES : (half + 1) * LANES] = lperm[half, pl.ds(pl.multiple_of(d * 16, 16), 16), :].astype(BF16)

    loop(0, SEQ, pack)

    loop(1, COLUMN, lambda i: a2_copy(i).wait_recv())
    loop(1, ROW, lambda i: b2_copy(i).wait_recv())

    def l_copy(i):
        return remote(gl_send.at[peer(i)], gl_recv.at[me], lsend.at[i], lrecv.at[me], peer(i))

    def l_arrival(i):
        return remote(gl_send.at[peer(i)], gl_recv.at[peer(i)], lsend.at[i], lrecv.at[peer(i)], peer(i))

    loop(1, SEQ, lambda i: l_copy(i).start())
    gl_recv[me] = gl_send[me]

    def unpack(d):
        rows = pl.ds(pl.multiple_of(d * 16, 16), 16)
        dz, dy = lax.div(d, ROW), lax.rem(d, ROW)
        fperm[0, rows, :] = filt_a[dz, dy].astype(F32)
        fperm[1, rows, :] = filt_b[dy, dz].astype(F32)

    loop(0, SEQ, unpack)
    for q in range(QUADS):
        parts = []
        for half in range(2):
            picked = [
                fperm[half, pl.ds(16 * first + OWN_TAPS * q + i, 8, stride=16), :]
                for i in range(OWN_TAPS)
                for first in range(0, SEQ, 8)
            ]
            parts.append(jnp.concatenate(picked, axis=0).astype(BF16))
        taps = jnp.concatenate(parts, axis=1)
        spec_h[:, WIDE * q : WIDE * (q + 1)] = dot(fw[:, ROWS + LTAPS :], taps) * (1.0 / HALF)

    @pl.when(has_right)
    def _():
        gm0_copy().wait_recv()

    def gf_copy():
        return remote(gf_send, gf_recv, gf_sem.at[0], gf_sem.at[1], left)

    my_piece = lax.rem(me + SEQ - FIRST_OWNER, SEQ)

    def owner(p):
        return lax.rem(p + FIRST_OWNER, SEQ)

    def s_copy(p):
        return remote(gs_part.at[p], gs_recv.at[me], ssend.at[p], srecv.at[me], owner(p))

    def s_arrival(i):
        return remote(gs_part.at[0], gs_recv.at[peer(i)], ssend.at[0], srecv.at[peer(i)], peer(i))

    def a_copy(d):
        return remote(gs_all.at[my_piece], gs_all.at[my_piece], asend.at[d], arecv.at[my_piece], d)

    def a_arrival(p):
        return remote(gs_all.at[p], gs_all.at[p], asend.at[0], arecv.at[p], owner(p))

    def short_grad(c):
        for s in range(3):
            totals = [None] * STAPS
            for first in range(0, ROWS, 64):
                grad = fs[s, c, pl.ds(first, 64), :]
                for j in range(STAPS):
                    term = jnp.sum((grad * xs[s, c, pl.ds(EDGE + first - j, 64), :]).reshape(8, 8, LANES), axis=0)
                    totals[j] = term if totals[j] is None else totals[j] + term
            rows = [jnp.sum(t, axis=0, keepdims=True) for t in totals] + [jnp.zeros((1, LANES), F32)]
            gs_part[3 * c + s] = jnp.concatenate(rows, axis=0)

    def main(q):
        @pl.when(has_right)
        def _():
            gm_copy(q).wait_recv()

        later = dot(fw[:, ROWS : ROWS + LTAPS], gmx[ROWS : ROWS + LTAPS, wide(q)])
        for first in range(0, HALF, 64):
            re, im = pl.ds(first, 64), pl.ds(HALF + first, 64)
            gc, gi = spec_g[re, wide(q)], spec_g[im, wide(q)]
            oc, oi = spec_gm[re, wide(q)], spec_gm[im, wide(q)]
            hc, hi = spec_h[re, wide(q)], spec_h[im, wide(q)]
            mc, mi = oc - later[first : first + 64], oi - later[HALF + first : HALF + first + 64]
            y1[re, :] = (gc * hc - gi * hi).astype(BF16)
            y1[im, :] = (gc * hi + gi * hc).astype(BF16)
            y2[re, :] = (mc * hc + mi * hi).astype(BF16)
            y2[im, :] = (mi * hc - mc * hi).astype(BF16)
        mixing = dot(iv[0:ROWS, :], y1[...])
        grad_gating = dot(iv[0:ROWS, :], y2[...])
        for half in range(2):
            c = 2 * q + half
            part = slice(half * LANES, (half + 1) * LANES)
            fs[0, c, 0:ROWS, :] = ov[:, lanes(c)].astype(F32) * mixing[:, part]
            fs[1, c, 0:ROWS, :] = grad_gating[:, part] * fkv[1, c]
            fs[2, c, 0:ROWS, :] = grad_gating[:, part] * fkv[0, c]

        for half in range(2):
            short_grad(2 * q + half)
            for s in range(3):
                piece = 3 * (2 * q + half) + s

                @pl.when(piece != my_piece)
                def _():
                    s_copy(piece).start()

                @pl.when(piece == my_piece)
                def _():
                    gs_recv[me] = gs_part[piece]

    loop(0, QUADS, main)

    fold(gf_stage, fs, 0, gf_send)

    @pl.when(has_left)
    def _():
        gf_copy().start()

    def back(c, first, count):
        for s in range(3):
            total = None
            for j in range(STAPS):
                term = sfv[s, j : j + 1, lanes(c)] * fs[s, c, pl.ds(first + j, count), :]
                total = term if total is None else total + term
            gp_v[s, pl.ds(first, count), lanes(c)] = total.astype(BF16)

    def back_bulk(c):
        for first, count in ((0, 64), (64, 64), (128, 64), (192, 48)):
            back(c, first, count)

    loop(0, CHUNKS, back_bulk)

    @pl.when(has_right)
    def _():
        gf_copy().wait_recv()

    unfold(gf_recv, gf_stage, fs, ROWS)

    def back_edge(c):
        back(c, ROWS - EDGE, EDGE)

    loop(0, CHUNKS, back_edge)

    def hand_out(d):
        @pl.when(d != me)
        def _():
            a_copy(d).start()

    @pl.when(my_piece < PIECES)
    def _():
        loop(1, SEQ, lambda i: s_arrival(i).wait_recv())
        total = gs_recv[0]
        for d in range(1, SEQ):
            total = total + gs_recv[d]
        gs_all[my_piece] = total
        loop(0, SEQ, hand_out)

    loop(1, SEQ, lambda i: l_arrival(i).wait_recv())
    total = gl_recv[0].astype(F32)
    for d in range(1, SEQ):
        total = total + gl_recv[d].astype(F32)
    gl_sum[...] = total * (1.0 / HALF)
    for q in range(QUADS):
        gl_out[:, WIDE * q : WIDE * (q + 1)] = gl_sum[OWN_TAPS * q : OWN_TAPS * (q + 1), :]

    @pl.when(has_right)
    def _():
        ph_copy().wait_send()
        loop(0, QUADS, lambda q: g_copy(q).wait_send())

    @pl.when(has_left)
    def _():
        loop(0, QUADS, lambda q: gm_copy(q).wait_send())
        gm0_copy().wait_send()
        gf_copy().wait_send()

    for i in range(1, ROW):
        a1_copy(i).wait_send()
        b2_copy(i).wait_send()
    for i in range(1, COLUMN):
        a2_copy(i).wait_send()
        b1_copy(i).wait_send()
    loop(1, SEQ, lambda i: l_copy(i).wait_send())

    def s_sent(p):
        @pl.when(p != my_piece)
        def _():
            s_copy(p).wait_send()

    loop(0, PIECES, s_sent)

    def a_sent(d):
        @pl.when(d != me)
        def _():
            a_copy(d).wait_send()

    @pl.when(my_piece < PIECES)
    def _():
        loop(0, SEQ, a_sent)

    def a_wait(p):
        @pl.when(p != my_piece)
        def _():
            a_arrival(p).wait_recv()

    loop(0, PIECES, a_wait)
    for s in range(3):
        for c in range(CHUNKS):
            gs_out[s, :, c * LANES : (c + 1) * LANES] = gs_all[3 * c + s, 0:STAPS, :]


def write_out(gp, gs, gl, gp_hbm, gs_hbm, gl_hbm, sems):
    copies = [pltpu.make_async_copy(src, dst, sems.at[n]) for n, (src, dst) in enumerate(((gp, gp_hbm), (gs, gs_hbm), (gl, gl_hbm)))]
    for copy in copies:
        copy.start()
    for copy in copies:
        copy.wait()


def on_device(projections, out_grad, short_filters, long_filter):
    forward, inverse = transforms()
    dma = pltpu.SemaphoreType.DMA
    vmem = pltpu.VMEM
    scratch = [
        vmem((3, ROWS, COLS), BF16),
        vmem((ROWS, COLS), BF16),
        vmem((3, STAPS, COLS), F32),
        vmem((OWN_TAPS, COLS), F32),
        vmem(forward.shape, BF16),
        vmem(inverse.shape, BF16),
        vmem((3, CHUNKS, EDGE + ROWS, LANES), F32),
        vmem((3, CHUNKS, ROWS + EDGE, LANES), F32),
        vmem((2, CHUNKS, ROWS, LANES), F32),
        vmem((LTAPS + ROWS, COLS), BF16),
        vmem((ROWS + LTAPS, COLS), BF16),
        vmem((CHUNKS + 1, EDGE, LANES), F32),
        vmem((EDGE, COLS + LANES), BF16),
        vmem((EDGE, COLS + LANES), BF16),
        vmem((CHUNKS + 1, EDGE, LANES), F32),
        vmem((EDGE, COLS + LANES), BF16),
        vmem((EDGE, COLS + LANES), BF16),
        vmem((COLUMN, ROW, 16, LANES), BF16),
        vmem((ROW, COLUMN, 16, LANES), BF16),
        vmem((2, SEQ * 16, LANES), F32),
        vmem((POINTS, COLS), F32),
        vmem((POINTS, COLS), F32),
        vmem((POINTS, COLS), F32),
        vmem((POINTS, WIDE), BF16),
        vmem((POINTS, WIDE), BF16),
        vmem((2, SEQ * 16, LANES), F32),
        vmem((SEQ, 16, WIDE), BF16),
        vmem((SEQ, 16, WIDE), BF16),
        vmem((16, WIDE), F32),
        vmem((PIECES, 8, LANES), F32),
        vmem((SEQ, 8, LANES), F32),
        vmem((PIECES, 8, LANES), F32),
        dma((8,)), dma((2,)), dma((2, QUADS)), dma((2, QUADS)), dma((2,)), dma((2,)),
        dma((SEQ,)), dma((SEQ,)), dma((SEQ,)), dma((SEQ,)), dma((PIECES,)), dma((SEQ,)), dma((SEQ,)), dma((SEQ,)),
    ]
    hbm = pl.BlockSpec(memory_space=pltpu.HBM)
    in_vmem = pl.BlockSpec(memory_space=pltpu.VMEM)
    operands = (projections, out_grad, short_filters, long_filter, jnp.asarray(forward), jnp.asarray(inverse))
    results = pl.pallas_call(
        kernel,
        out_shape=(
            pltpu.VMEM(projections.shape, BF16),
            pltpu.VMEM(short_filters.shape, F32),
            pltpu.VMEM(long_filter.shape, F32),
        ),
        in_specs=[hbm] * len(operands),
        out_specs=(in_vmem,) * 3,
        scratch_shapes=scratch,
        compiler_params=pltpu.CompilerParams(collective_id=0, has_side_effects=True, vmem_limit_bytes=50 << 20),
    )(*[pltpu.with_memory_space_constraint(operand, pltpu.HBM) for operand in operands])
    return pl.pallas_call(
        write_out,
        out_shape=tuple(jax.ShapeDtypeStruct(r.shape, r.dtype) for r in results),
        in_specs=[in_vmem] * 3,
        out_specs=(hbm,) * 3,
        scratch_shapes=[dma((3,))],
    )(*[pltpu.with_memory_space_constraint(result, pltpu.VMEM) for result in results])


def solution(mesh):
    in_specs = (
        P(None, "seq", "tensor"),
        P("seq", "tensor"),
        P(None, None, "tensor"),
        P("seq", "tensor"),
    )
    out_specs = (P(None, "seq", "tensor"), P(None, None, "tensor"), P("seq", "tensor"))
    return jax.shard_map(on_device, mesh=mesh, in_specs=in_specs, out_specs=out_specs, check_vma=False)
```

```python
import jax
import jax.numpy as jnp
import ml_dtypes
import numpy as np
from jax import lax
from jax.experimental import pallas as pl
from jax.experimental.pallas import tpu as pltpu
from jax.sharding import PartitionSpec as P

MESH = pl.DeviceIdType.MESH
F32 = jnp.float32
BF16 = jnp.bfloat16

STAPS = 7
LTAPS = 128
ROWS = 256
COLS = 1024
LANES = 128
CHUNKS = COLS // LANES
WIDE = 256
QUADS = COLS // WIDE
SEQ = 32
OWN_TAPS = LTAPS // SEQ
POINTS = ROWS + LTAPS
HALF = POINTS // 2
EDGE = 16
PIECES = 3 * QUADS
ROW = 4
COLUMN = 8
FIRST_OWNER = 30
HALO = STAPS - 1
SHARE = LTAPS // ROW


def transforms():
    freqs = 2.0 * np.pi * (np.arange(HALF) + 0.5) / POINTS

    def rows(times):
        angles = np.outer(freqs, times)
        return np.concatenate([np.cos(angles), np.sin(angles)], axis=0)

    own = rows(np.arange(ROWS))
    prior = rows(np.arange(-LTAPS, 0))
    tap_order = np.arange(LTAPS).reshape(SEQ, OWN_TAPS).T.reshape(-1)
    taps = rows(tap_order)
    own_rest = own - own.astype(ml_dtypes.bfloat16).astype(np.float64)
    forward = np.concatenate([own, prior, taps, own_rest], axis=1).astype(ml_dtypes.bfloat16)
    grad_order = np.arange(LTAPS).reshape(COLUMN, ROW, OWN_TAPS).transpose(1, 2, 0).reshape(-1)
    inverse = np.concatenate([own.T, rows(grad_order).T], axis=0).astype(ml_dtypes.bfloat16)
    return forward, inverse


def lanes(c):
    return pl.ds(pl.multiple_of(c * LANES, LANES), LANES)


def wide(q):
    return pl.ds(pl.multiple_of(q * WIDE, WIDE), WIDE)


def dot(a, b):
    return jnp.dot(a, b, preferred_element_type=F32)


def kernel(
    proj_hbm, og_hbm, sf_hbm, lf_hbm, fw_hbm, iv_hbm,
    gp_v, gs_out, gl_out,
    pv, ov, sfv, lfv, fw, iv,
    xs, fs, fkv, gx, gmx, ph_stage, ph_send, ph_recv, gf_stage, gf_send, gf_recv,
    filt_a, filt_b, fperm, spec_g, spec_gm, spec_h, y1, y2,
    lperm, gl_row_send, gl_row_recv, gl_send, gl_recv, gl_sum, gs_rows, gs_part, gs_recv, gs_all,
    load_sem, ph_sem, g_sem, gm_sem, gm0_sem, gf_sem,
    fsend, frecv, msend, mrecv, lsend, lrecv, ssend, srecv, asend, arecv,
):
    me = lax.axis_index("seq")
    right, left = lax.rem(me + 1, SEQ), lax.rem(me + SEQ - 1, SEQ)
    has_left, has_right = me > 0, me < SEQ - 1

    def peer(i):
        return lax.rem(me + i, SEQ)

    def remote(src, dst, send_sem, recv_sem, to):
        return pltpu.make_async_remote_copy(
            src_ref=src, dst_ref=dst, send_sem=send_sem, recv_sem=recv_sem,
            device_id={"seq": to}, device_id_type=MESH,
        )

    def loop(low, high, body):
        lax.fori_loop(low, high, lambda i, _: (body(i), 0)[1], 0)

    y, z = lax.rem(me, ROW), lax.div(me, ROW)

    def in_row(i):
        return z * ROW + lax.rem(y + i, ROW)

    def in_column(i):
        return lax.rem(z + i, COLUMN) * ROW + y

    barrier = pltpu.get_barrier_semaphore()
    greeted = [left, right] + [in_row(i) for i in range(1, ROW)] + [in_column(i) for i in range(1, COLUMN)]
    for other in greeted:
        pl.semaphore_signal(barrier, inc=1, device_id={"seq": other}, device_id_type=MESH)

    loads = [
        pltpu.make_async_copy(src, dst, load_sem.at[n])
        for n, (src, dst) in enumerate(
            [
                (sf_hbm, sfv), (proj_hbm.at[1], pv.at[1]), (proj_hbm.at[2], pv.at[2]), (proj_hbm.at[0], pv.at[0]),
                (og_hbm, ov), (lf_hbm, lfv), (fw_hbm, fw), (iv_hbm, iv),
            ]
        )
    ]
    for load in loads:
        load.start()

    def feature(s, c, first, count):
        total = None
        for j in range(STAPS):
            term = sfv[s, j : j + 1, lanes(c)] * xs[s, c, pl.ds(EDGE + first - j, count), :]
            total = term if total is None else total + term
        return total

    def gated(c, first, count):
        k, v = feature(1, c, first, count), feature(2, c, first, count)
        fkv[0, c, pl.ds(first, count), :] = k
        fkv[1, c, pl.ds(first, count), :] = v
        gx[pl.ds(LTAPS + first, count), lanes(c)] = (k * v).astype(BF16)

    def mixed(c, first, count):
        cotangent = ov[pl.ds(first, count), lanes(c)].astype(F32)
        gmx[pl.ds(first, count), lanes(c)] = (cotangent * feature(0, c, first, count)).astype(BF16)

    def widen(s, c):
        xs[s, c, pl.ds(EDGE, ROWS), :] = pv[s, :, lanes(c)].astype(F32)

    for load in loads[:3]:
        load.wait()

    def tail(c):
        widen(1, c)
        widen(2, c)
        for first in (128, 192):
            gated(c, first, 64)

    loop(0, CHUNKS, tail)
    loads[3].wait()
    loads[4].wait()

    def head(c):
        widen(0, c)
        for first, count in ((16, 48), (64, 64)):
            mixed(c, first, count)

    loop(0, CHUNKS, head)
    loads[5].wait()
    for q in range(QUADS):
        lperm[0, OWN_TAPS * q : OWN_TAPS * (q + 1), :] = lfv[:, WIDE * q : WIDE * q + LANES]
        lperm[1, OWN_TAPS * q : OWN_TAPS * (q + 1), :] = lfv[:, WIDE * q + LANES : WIDE * (q + 1)]
    filt_a[z, y] = lperm[0, 0:16, :].astype(BF16)
    filt_b[y, z] = lperm[1, 0:16, :].astype(BF16)

    def fold(stage, source, first, packed):
        for c in range(CHUNKS):
            stage[c, 0:6, :] = source[0, c, first : first + 6, :]
            stage[c, 6:12, :] = source[1, c, first : first + 6, :]
            stage[c, 12:16, :] = source[2, c, first : first + 4, :]
            stage[CHUNKS, 2 * c : 2 * c + 2, :] = source[2, c, first + 4 : first + 6, :]
        for c in range(CHUNKS + 1):
            packed[:, LANES * c : LANES * (c + 1)] = stage[c].astype(BF16)

    def unfold(packed, stage, target, first):
        for c in range(CHUNKS + 1):
            stage[c] = packed[:, LANES * c : LANES * (c + 1)].astype(F32)
        for c in range(CHUNKS):
            target[0, c, first : first + 6, :] = stage[c, 0:6, :]
            target[1, c, first : first + 6, :] = stage[c, 6:12, :]
            target[2, c, first : first + 4, :] = stage[c, 12:16, :]
            target[2, c, first + 4 : first + 6, :] = stage[CHUNKS, 2 * c : 2 * c + 2, :]

    fold(ph_stage, xs, EDGE + ROWS - HALO, ph_send)

    pl.semaphore_wait(barrier, len(greeted))

    def ph_copy():
        return remote(ph_send, ph_recv, ph_sem.at[0], ph_sem.at[1], right)

    def g_copy(q):
        return remote(gx.at[pl.ds(ROWS, LTAPS), wide(q)], gx.at[pl.ds(0, LTAPS), wide(q)], g_sem.at[0, q], g_sem.at[1, q], right)

    def gm_copy(q):
        return remote(
            gmx.at[pl.ds(EDGE, LTAPS - EDGE), wide(q)], gmx.at[pl.ds(ROWS + EDGE, LTAPS - EDGE), wide(q)],
            gm_sem.at[0, q], gm_sem.at[1, q], left,
        )

    def gm0_copy():
        return remote(gmx.at[pl.ds(0, EDGE), :], gmx.at[pl.ds(ROWS, EDGE), :], gm0_sem.at[0], gm0_sem.at[1], left)

    def a1_copy(i):
        return remote(filt_a.at[z, y], filt_a.at[z, y], fsend.at[i], frecv.at[i], in_row(i))

    def a2_copy(i):
        return remote(filt_a.at[z], filt_a.at[z], fsend.at[ROW + i], frecv.at[ROW + i], in_column(i))

    def b1_copy(i):
        return remote(filt_b.at[y, z], filt_b.at[y, z], fsend.at[12 + i], frecv.at[12 + i], in_column(i))

    def b2_copy(i):
        return remote(filt_b.at[y], filt_b.at[y], fsend.at[20 + i], frecv.at[20 + i], in_row(i))

    loop(1, ROW, lambda i: a1_copy(i).start())
    loop(1, COLUMN, lambda i: b1_copy(i).start())

    @pl.when(has_right)
    def _():
        ph_copy().start()
        loop(0, QUADS, lambda q: g_copy(q).start())

    @pl.when(has_left)
    def _():
        loop(0, QUADS, lambda q: gm_copy(q).start())

    def rest(c):
        for first, count in ((16, 48), (64, 64)):
            gated(c, first, count)
        for first in (128, 192):
            mixed(c, first, 64)

    loop(0, CHUNKS, rest)

    loop(1, ROW, lambda i: a1_copy(i).wait_recv())
    loop(1, COLUMN, lambda i: a2_copy(i).start())

    @pl.when(has_left)
    def _():
        ph_copy().wait_recv()

    @pl.when(jnp.logical_not(has_left))
    def _():
        ph_recv[...] = jnp.zeros_like(ph_recv)
        gx[0:LTAPS, :] = jnp.zeros((LTAPS, COLS), BF16)

    @pl.when(jnp.logical_not(has_right))
    def _():
        gmx[ROWS : ROWS + LTAPS, :] = jnp.zeros((LTAPS, COLS), BF16)
        gf_recv[...] = jnp.zeros_like(gf_recv)

    unfold(ph_recv, ph_stage, xs, EDGE - HALO)

    def edge(c):
        mixed(c, 0, EDGE)
        gated(c, 0, EDGE)

    loop(0, CHUNKS, edge)

    @pl.when(has_left)
    def _():
        gm0_copy().start()

    loads[6].wait()
    loads[7].wait()

    def own_spectra(q):
        for spec, values in ((spec_g, gx[LTAPS : LTAPS + ROWS, wide(q)]), (spec_gm, gmx[0:ROWS, wide(q)])):
            spec[:, wide(q)] = dot(fw[:, 0:ROWS], values) + dot(fw[:, 2 * ROWS : 3 * ROWS], values)

    loop(0, 2, own_spectra)

    loop(1, COLUMN, lambda i: b1_copy(i).wait_recv())
    loop(1, ROW, lambda i: b2_copy(i).start())

    loop(2, QUADS, own_spectra)

    def m_copy(q, i):
        return remote(
            gl_row_send.at[q, lax.rem(y + i, ROW)], gl_row_recv.at[q, i], msend.at[q, i], mrecv.at[q, i], in_row(i)
        )

    for q in range(QUADS):

        @pl.when(has_left)
        def _():
            g_copy(q).wait_recv()

        spec_g[:, WIDE * q : WIDE * (q + 1)] += dot(fw[:, ROWS : ROWS + LTAPS], gx[0:LTAPS, WIDE * q : WIDE * (q + 1)])
        for first in range(0, HALF, 64):
            re, im = pl.ds(first, 64), pl.ds(HALF + first, 64)
            cols = pl.ds(WIDE * q, WIDE)
            gc, gi = spec_g[re, cols], spec_g[im, cols]
            oc, oi = spec_gm[re, cols], spec_gm[im, cols]
            y1[re, :] = (oc * gc + oi * gi).astype(BF16)
            y1[im, :] = (oi * gc - oc * gi).astype(BF16)
        partial = dot(iv[ROWS:, :], y1[...]).astype(BF16)
        for row in range(ROW):
            gl_row_send[q, row] = partial[SHARE * row : SHARE * (row + 1), :]
        loop(1, ROW, lambda i: m_copy(q, i).start())

    @pl.when(has_right)
    def _():
        gm0_copy().wait_recv()

    for q in range(QUADS):

        @pl.when(has_right)
        def _():
            gm_copy(q).wait_recv()

        spec_gm[:, WIDE * q : WIDE * (q + 1)] -= dot(
            fw[:, ROWS : ROWS + LTAPS], gmx[ROWS : ROWS + LTAPS, WIDE * q : WIDE * (q + 1)]
        )

    loop(1, COLUMN, lambda i: a2_copy(i).wait_recv())
    loop(1, ROW, lambda i: b2_copy(i).wait_recv())

    def unpack(d):
        rows = pl.ds(pl.multiple_of(d * 16, 16), 16)
        dz, dy = lax.div(d, ROW), lax.rem(d, ROW)
        fperm[0, rows, :] = filt_a[dz, dy].astype(F32)
        fperm[1, rows, :] = filt_b[dy, dz].astype(F32)

    loop(0, SEQ, unpack)
    for q in range(QUADS):
        parts = []
        for half in range(2):
            picked = [
                fperm[half, pl.ds(16 * first + OWN_TAPS * q + i, 8, stride=16), :]
                for i in range(OWN_TAPS)
                for first in range(0, SEQ, 8)
            ]
            parts.append(jnp.concatenate(picked, axis=0).astype(BF16))
        taps = jnp.concatenate(parts, axis=1)
        spec_h[:, WIDE * q : WIDE * (q + 1)] = dot(fw[:, ROWS + LTAPS : 2 * ROWS], taps) * (1.0 / HALF)

    def gf_copy():
        return remote(gf_send, gf_recv, gf_sem.at[0], gf_sem.at[1], left)

    my_piece = lax.rem(me + SEQ - FIRST_OWNER, SEQ)

    def owner(p):
        return lax.rem(p + FIRST_OWNER, SEQ)

    def s_copy(p):
        return remote(gs_part.at[p], gs_recv.at[me], ssend.at[p], srecv.at[me], owner(p))

    def s_arrival(i):
        return remote(gs_part.at[0], gs_recv.at[peer(i)], ssend.at[0], srecv.at[peer(i)], peer(i))

    def a_copy(d):
        return remote(gs_all.at[my_piece], gs_all.at[my_piece], asend.at[d], arecv.at[my_piece], d)

    def a_arrival(p):
        return remote(gs_all.at[p], gs_all.at[p], asend.at[0], arecv.at[p], owner(p))

    def short_grad(q, half):
        c = 2 * q + half
        for s in range(3):
            totals = [None] * STAPS
            for first in range(0, ROWS, 64):
                grad = fs[s, c, pl.ds(first, 64), :]
                for j in range(STAPS):
                    term = jnp.sum((grad * xs[s, c, pl.ds(EDGE + first - j, 64), :]).reshape(8, 8, LANES), axis=0)
                    totals[j] = term if totals[j] is None else totals[j] + term
            rows = jnp.concatenate([jnp.sum(t, axis=0, keepdims=True) for t in totals], axis=0)
            start = STAPS * (3 * half + s)
            gs_rows[q, start : start + STAPS, :] = rows

    def main(q):
        for first in range(0, HALF, 64):
            re, im = pl.ds(first, 64), pl.ds(HALF + first, 64)
            gc, gi = spec_g[re, wide(q)], spec_g[im, wide(q)]
            mc, mi = spec_gm[re, wide(q)], spec_gm[im, wide(q)]
            hc, hi = spec_h[re, wide(q)], spec_h[im, wide(q)]
            y1[re, :] = (gc * hc - gi * hi).astype(BF16)
            y1[im, :] = (gc * hi + gi * hc).astype(BF16)
            y2[re, :] = (mc * hc + mi * hi).astype(BF16)
            y2[im, :] = (mi * hc - mc * hi).astype(BF16)
        mixing = dot(iv[0:ROWS, :], y1[...])
        grad_gating = dot(iv[0:ROWS, :], y2[...])
        for half in range(2):
            c = 2 * q + half
            part = slice(half * LANES, (half + 1) * LANES)
            fs[0, c, 0:ROWS, :] = ov[:, lanes(c)].astype(F32) * mixing[:, part]
            fs[1, c, 0:ROWS, :] = grad_gating[:, part] * fkv[1, c]
            fs[2, c, 0:ROWS, :] = grad_gating[:, part] * fkv[0, c]

        gs_rows[q, 40:48, :] = jnp.zeros((8, LANES), F32)
        for half in range(2):
            short_grad(q, half)
        for k in range(3):
            piece = 3 * q + k
            gs_part[piece] = gs_rows[q, 16 * k : 16 * (k + 1), :].astype(BF16)

            @pl.when(piece != my_piece)
            def _():
                s_copy(piece).start()

            @pl.when(piece == my_piece)
            def _():
                gs_recv[me] = gs_part[piece]

    loop(0, QUADS, main)

    fold(gf_stage, fs, 0, gf_send)

    @pl.when(has_left)
    def _():
        gf_copy().start()

    def l_copy(i):
        return remote(gl_send.at[lax.rem(z + i, COLUMN)], gl_recv.at[i], lsend.at[i], lrecv.at[i], in_column(i))

    for q in range(QUADS):
        loop(1, ROW, lambda i: m_copy(q, i).wait_recv())
        total = gl_row_send[q, y].astype(F32)
        for i in range(1, ROW):
            total = total + gl_row_recv[q, i].astype(F32)
        for half in range(2):
            for i in range(OWN_TAPS):
                rows = total[COLUMN * i : COLUMN * (i + 1), half * LANES : (half + 1) * LANES]
                lperm[half, pl.ds(OWN_TAPS * q + i, COLUMN, stride=16), :] = rows
    for d in range(COLUMN):
        for half in range(2):
            gl_send[d, :, half * LANES : (half + 1) * LANES] = lperm[half, 16 * d : 16 * (d + 1), :].astype(BF16)
    loop(1, COLUMN, lambda i: l_copy(i).start())
    gl_recv[0] = gl_send[z]

    def back(c, first, count):
        for s in range(3):
            total = None
            for j in range(STAPS):
                term = sfv[s, j : j + 1, lanes(c)] * fs[s, c, pl.ds(first + j, count), :]
                total = term if total is None else total + term
            gp_v[s, pl.ds(first, count), lanes(c)] = total.astype(BF16)

    def back_bulk(c):
        for first, count in ((0, 64), (64, 64), (128, 64), (192, 48)):
            back(c, first, count)

    loop(0, CHUNKS, back_bulk)

    @pl.when(has_right)
    def _():
        gf_copy().wait_recv()

    unfold(gf_recv, gf_stage, fs, ROWS)

    def back_edge(c):
        back(c, ROWS - EDGE, EDGE)

    loop(0, CHUNKS, back_edge)

    def hand_out(d):
        @pl.when(d != me)
        def _():
            a_copy(d).start()

    @pl.when(my_piece < PIECES)
    def _():
        loop(1, SEQ, lambda i: s_arrival(i).wait_recv())
        total = gs_recv[0].astype(F32)
        for d in range(1, SEQ):
            total = total + gs_recv[d].astype(F32)
        gs_all[my_piece] = total.astype(BF16)
        loop(0, SEQ, hand_out)

    loop(1, COLUMN, lambda i: l_copy(i).wait_recv())
    total = gl_recv[0].astype(F32)
    for d in range(1, COLUMN):
        total = total + gl_recv[d].astype(F32)
    gl_sum[...] = total * (1.0 / HALF)
    for q in range(QUADS):
        gl_out[:, WIDE * q : WIDE * (q + 1)] = gl_sum[OWN_TAPS * q : OWN_TAPS * (q + 1), :]

    @pl.when(has_right)
    def _():
        ph_copy().wait_send()
        loop(0, QUADS, lambda q: g_copy(q).wait_send())

    @pl.when(has_left)
    def _():
        loop(0, QUADS, lambda q: gm_copy(q).wait_send())
        gm0_copy().wait_send()
        gf_copy().wait_send()

    for i in range(1, ROW):
        a1_copy(i).wait_send()
        b2_copy(i).wait_send()
    for i in range(1, COLUMN):
        a2_copy(i).wait_send()
        b1_copy(i).wait_send()
    loop(1, COLUMN, lambda i: l_copy(i).wait_send())
    for q in range(QUADS):
        loop(1, ROW, lambda i: m_copy(q, i).wait_send())

    def s_sent(p):
        @pl.when(p != my_piece)
        def _():
            s_copy(p).wait_send()

    loop(0, PIECES, s_sent)

    def a_sent(d):
        @pl.when(d != me)
        def _():
            a_copy(d).wait_send()

    @pl.when(my_piece < PIECES)
    def _():
        loop(0, SEQ, a_sent)

    def a_wait(p):
        @pl.when(p != my_piece)
        def _():
            a_arrival(p).wait_recv()

    loop(0, PIECES, a_wait)
    for q in range(QUADS):
        for k in range(3):
            gs_rows[q, 16 * k : 16 * (k + 1), :] = gs_all[3 * q + k].astype(F32)
        for half in range(2):
            for s in range(3):
                start, c = STAPS * (3 * half + s), 2 * q + half
                gs_out[s, :, c * LANES : (c + 1) * LANES] = gs_rows[q, start : start + STAPS, :]


def write_out(gp, gs, gl, gp_hbm, gs_hbm, gl_hbm, sems):
    copies = [pltpu.make_async_copy(src, dst, sems.at[n]) for n, (src, dst) in enumerate(((gp, gp_hbm), (gs, gs_hbm), (gl, gl_hbm)))]
    for copy in copies:
        copy.start()
    for copy in copies:
        copy.wait()


def on_device(projections, out_grad, short_filters, long_filter):
    forward, inverse = transforms()
    dma = pltpu.SemaphoreType.DMA
    vmem = pltpu.VMEM
    scratch = [
        vmem((3, ROWS, COLS), BF16),
        vmem((ROWS, COLS), BF16),
        vmem((3, STAPS, COLS), F32),
        vmem((OWN_TAPS, COLS), F32),
        vmem(forward.shape, BF16),
        vmem(inverse.shape, BF16),
        vmem((3, CHUNKS, EDGE + ROWS, LANES), F32),
        vmem((3, CHUNKS, ROWS + EDGE, LANES), F32),
        vmem((2, CHUNKS, ROWS, LANES), F32),
        vmem((LTAPS + ROWS, COLS), BF16),
        vmem((ROWS + LTAPS, COLS), BF16),
        vmem((CHUNKS + 1, EDGE, LANES), F32),
        vmem((EDGE, COLS + LANES), BF16),
        vmem((EDGE, COLS + LANES), BF16),
        vmem((CHUNKS + 1, EDGE, LANES), F32),
        vmem((EDGE, COLS + LANES), BF16),
        vmem((EDGE, COLS + LANES), BF16),
        vmem((COLUMN, ROW, 16, LANES), BF16),
        vmem((ROW, COLUMN, 16, LANES), BF16),
        vmem((2, SEQ * 16, LANES), F32),
        vmem((POINTS, COLS), F32),
        vmem((POINTS, COLS), F32),
        vmem((POINTS, COLS), F32),
        vmem((POINTS, WIDE), BF16),
        vmem((POINTS, WIDE), BF16),
        vmem((2, SEQ * 16, LANES), F32),
        vmem((QUADS, ROW, SHARE, WIDE), BF16),
        vmem((QUADS, ROW, SHARE, WIDE), BF16),
        vmem((COLUMN, 16, WIDE), BF16),
        vmem((COLUMN, 16, WIDE), BF16),
        vmem((16, WIDE), F32),
        vmem((QUADS, 48, LANES), F32),
        vmem((PIECES, 16, LANES), BF16),
        vmem((SEQ, 16, LANES), BF16),
        vmem((PIECES, 16, LANES), BF16),
        dma((8,)), dma((2,)), dma((2, QUADS)), dma((2, QUADS)), dma((2,)), dma((2,)),
        dma((SEQ,)), dma((SEQ,)), dma((QUADS, ROW)), dma((QUADS, ROW)), dma((COLUMN,)), dma((COLUMN,)), dma((PIECES,)), dma((SEQ,)), dma((SEQ,)), dma((SEQ,)),
    ]
    hbm = pl.BlockSpec(memory_space=pltpu.HBM)
    in_vmem = pl.BlockSpec(memory_space=pltpu.VMEM)
    operands = (projections, out_grad, short_filters, long_filter, jnp.asarray(forward), jnp.asarray(inverse))
    results = pl.pallas_call(
        kernel,
        out_shape=(
            pltpu.VMEM(projections.shape, BF16),
            pltpu.VMEM(short_filters.shape, F32),
            pltpu.VMEM(long_filter.shape, F32),
        ),
        in_specs=[hbm] * len(operands),
        out_specs=(in_vmem,) * 3,
        scratch_shapes=scratch,
        compiler_params=pltpu.CompilerParams(collective_id=0, has_side_effects=True, vmem_limit_bytes=50 << 20),
    )(*[pltpu.with_memory_space_constraint(operand, pltpu.HBM) for operand in operands])
    return pl.pallas_call(
        write_out,
        out_shape=tuple(jax.ShapeDtypeStruct(r.shape, r.dtype) for r in results),
        in_specs=[in_vmem] * 3,
        out_specs=(hbm,) * 3,
        scratch_shapes=[dma((3,))],
    )(*[pltpu.with_memory_space_constraint(result, pltpu.VMEM) for result in results])


def solution(mesh):
    in_specs = (
        P(None, "seq", "tensor"),
        P("seq", "tensor"),
        P(None, None, "tensor"),
        P("seq", "tensor"),
    )
    out_specs = (P(None, "seq", "tensor"), P(None, None, "tensor"), P("seq", "tensor"))
    return jax.shard_map(on_device, mesh=mesh, in_specs=in_specs, out_specs=out_specs, check_vma=False)
```

```python
import jax
import jax.numpy as jnp
import ml_dtypes
import numpy as np
from jax import lax
from jax.experimental import pallas as pl
from jax.experimental.pallas import tpu as pltpu
from jax.sharding import PartitionSpec as P

MESH = pl.DeviceIdType.MESH
F32 = jnp.float32
BF16 = jnp.bfloat16

STAPS = 7
LTAPS = 128
ROWS = 256
COLS = 1024
LANES = 128
CHUNKS = COLS // LANES
WIDE = 256
QUADS = COLS // WIDE
SEQ = 32
OWN_TAPS = LTAPS // SEQ
POINTS = ROWS + LTAPS
HALF = POINTS // 2
EDGE = 16
PIECES = 3 * QUADS
ROW = 4
COLUMN = 8
FIRST_OWNER = 30
HALO = STAPS - 1
SHARE = LTAPS // ROW


def transforms():
    freqs = 2.0 * np.pi * (np.arange(HALF) + 0.5) / POINTS

    def rows(times):
        angles = np.outer(freqs, times)
        return np.concatenate([np.cos(angles), np.sin(angles)], axis=0)

    own = rows(np.arange(ROWS))
    prior = rows(np.arange(-LTAPS, 0))
    tap_order = np.arange(LTAPS).reshape(SEQ, OWN_TAPS).T.reshape(-1)
    taps = rows(tap_order)
    own_rest = own - own.astype(ml_dtypes.bfloat16).astype(np.float64)
    forward = np.concatenate([own, prior, taps, own_rest], axis=1).astype(ml_dtypes.bfloat16)
    grad_order = np.arange(LTAPS).reshape(COLUMN, ROW, OWN_TAPS).transpose(1, 2, 0).reshape(-1)
    inverse = np.concatenate([own.T, rows(grad_order).T], axis=0).astype(ml_dtypes.bfloat16)
    return forward, inverse


def lanes(c):
    return pl.ds(pl.multiple_of(c * LANES, LANES), LANES)


def wide(q):
    return pl.ds(pl.multiple_of(q * WIDE, WIDE), WIDE)


def dot(a, b):
    return jnp.dot(a, b, preferred_element_type=F32)


def kernel(
    proj_hbm, og_hbm, sf_hbm, lf_hbm, fw_hbm, iv_hbm,
    gp_v, gs_out, gl_out,
    pv, ov, sfv, lfv, fw, iv,
    xs, fs, fkv, gx, gmx, ph_stage, ph_send, ph_recv, gf_stage, gf_send, gf_recv,
    filt_a, filt_b, fperm, spec_g, spec_gm, spec_h, y1, y2,
    lperm, gl_row_send, gl_row_recv, gl_send, gl_recv, gl_sum, gs_rows, gs_part, gs_recv, gs_all,
    load_sem, ph_sem, g_sem, gm_sem, gm0_sem, gf_sem,
    fsend, frecv, msend, mrecv, lsend, lrecv, ssend, srecv, asend, arecv,
):
    me = lax.axis_index("seq")
    right, left = lax.rem(me + 1, SEQ), lax.rem(me + SEQ - 1, SEQ)
    has_left, has_right = me > 0, me < SEQ - 1

    def peer(i):
        return lax.rem(me + i, SEQ)

    def remote(src, dst, send_sem, recv_sem, to):
        return pltpu.make_async_remote_copy(
            src_ref=src, dst_ref=dst, send_sem=send_sem, recv_sem=recv_sem,
            device_id={"seq": to}, device_id_type=MESH,
        )

    def loop(low, high, body):
        lax.fori_loop(low, high, lambda i, _: (body(i), 0)[1], 0)

    y, z = lax.rem(me, ROW), lax.div(me, ROW)

    def in_row(i):
        return z * ROW + lax.rem(y + i, ROW)

    def in_column(i):
        return lax.rem(z + i, COLUMN) * ROW + y

    barrier = pltpu.get_barrier_semaphore()
    greeted = [left, right] + [in_row(i) for i in range(1, ROW)] + [in_column(i) for i in range(1, COLUMN)]
    for other in greeted:
        pl.semaphore_signal(barrier, inc=1, device_id={"seq": other}, device_id_type=MESH)

    loads = [
        pltpu.make_async_copy(src, dst, load_sem.at[n])
        for n, (src, dst) in enumerate(
            [
                (sf_hbm, sfv), (proj_hbm.at[1], pv.at[1]), (proj_hbm.at[2], pv.at[2]), (proj_hbm.at[0], pv.at[0]),
                (og_hbm, ov), (lf_hbm, lfv), (fw_hbm, fw), (iv_hbm, iv),
            ]
        )
    ]
    for load in loads:
        load.start()

    def feature(s, c, first, count):
        total = None
        for j in range(STAPS):
            term = sfv[s, j : j + 1, lanes(c)] * xs[s, c, pl.ds(EDGE + first - j, count), :]
            total = term if total is None else total + term
        return total

    def gated(c, first, count):
        k, v = feature(1, c, first, count), feature(2, c, first, count)
        fkv[0, c, pl.ds(first, count), :] = k
        fkv[1, c, pl.ds(first, count), :] = v
        gx[pl.ds(LTAPS + first, count), lanes(c)] = (k * v).astype(BF16)

    def mixed(c, first, count):
        cotangent = ov[pl.ds(first, count), lanes(c)].astype(F32)
        gmx[pl.ds(first, count), lanes(c)] = (cotangent * feature(0, c, first, count)).astype(BF16)

    def widen(s, c):
        xs[s, c, pl.ds(EDGE, ROWS), :] = pv[s, :, lanes(c)].astype(F32)

    for load in loads[:3]:
        load.wait()

    def tail(c):
        widen(1, c)
        widen(2, c)
        for first in (128, 192):
            gated(c, first, 64)

    loop(0, CHUNKS, tail)
    loads[3].wait()
    loads[4].wait()

    def head(c):
        widen(0, c)
        for first, count in ((16, 48), (64, 64)):
            mixed(c, first, count)

    loop(0, CHUNKS, head)
    loads[5].wait()
    for q in range(QUADS):
        lperm[0, OWN_TAPS * q : OWN_TAPS * (q + 1), :] = lfv[:, WIDE * q : WIDE * q + LANES]
        lperm[1, OWN_TAPS * q : OWN_TAPS * (q + 1), :] = lfv[:, WIDE * q + LANES : WIDE * (q + 1)]
    filt_a[z, y] = lperm[0, 0:16, :].astype(BF16)
    filt_b[y, z] = lperm[1, 0:16, :].astype(BF16)

    def fold(stage, source, first, packed):
        for c in range(CHUNKS):
            stage[c, 0:6, :] = source[0, c, first : first + 6, :]
            stage[c, 6:12, :] = source[1, c, first : first + 6, :]
            stage[c, 12:16, :] = source[2, c, first : first + 4, :]
            stage[CHUNKS, 2 * c : 2 * c + 2, :] = source[2, c, first + 4 : first + 6, :]
        for c in range(CHUNKS + 1):
            packed[:, LANES * c : LANES * (c + 1)] = stage[c].astype(BF16)

    def unfold(packed, stage, target, first):
        for c in range(CHUNKS + 1):
            stage[c] = packed[:, LANES * c : LANES * (c + 1)].astype(F32)
        for c in range(CHUNKS):
            target[0, c, first : first + 6, :] = stage[c, 0:6, :]
            target[1, c, first : first + 6, :] = stage[c, 6:12, :]
            target[2, c, first : first + 4, :] = stage[c, 12:16, :]
            target[2, c, first + 4 : first + 6, :] = stage[CHUNKS, 2 * c : 2 * c + 2, :]

    fold(ph_stage, xs, EDGE + ROWS - HALO, ph_send)

    pl.semaphore_wait(barrier, len(greeted))

    def ph_copy():
        return remote(ph_send, ph_recv, ph_sem.at[0], ph_sem.at[1], right)

    def g_copy(q):
        return remote(gx.at[pl.ds(ROWS, LTAPS), wide(q)], gx.at[pl.ds(0, LTAPS), wide(q)], g_sem.at[0, q], g_sem.at[1, q], right)

    def gm_copy(q):
        return remote(
            gmx.at[pl.ds(EDGE, LTAPS - EDGE), wide(q)], gmx.at[pl.ds(ROWS + EDGE, LTAPS - EDGE), wide(q)],
            gm_sem.at[0, q], gm_sem.at[1, q], left,
        )

    def gm0_copy():
        return remote(gmx.at[pl.ds(0, EDGE), :], gmx.at[pl.ds(ROWS, EDGE), :], gm0_sem.at[0], gm0_sem.at[1], left)

    def a1_copy(i):
        return remote(filt_a.at[z, y], filt_a.at[z, y], fsend.at[i], frecv.at[i], in_row(i))

    def a2_copy(i):
        return remote(filt_a.at[z], filt_a.at[z], fsend.at[ROW + i], frecv.at[ROW + i], in_column(i))

    def b1_copy(i):
        return remote(filt_b.at[y, z], filt_b.at[y, z], fsend.at[12 + i], frecv.at[12 + i], in_column(i))

    def b2_copy(i):
        return remote(filt_b.at[y], filt_b.at[y], fsend.at[20 + i], frecv.at[20 + i], in_row(i))

    loop(1, ROW, lambda i: a1_copy(i).start())
    loop(1, COLUMN, lambda i: b1_copy(i).start())

    @pl.when(has_right)
    def _():
        ph_copy().start()
        loop(0, QUADS, lambda q: g_copy(q).start())

    @pl.when(has_left)
    def _():
        loop(0, QUADS, lambda q: gm_copy(q).start())

    def rest(c):
        for first, count in ((16, 48), (64, 64)):
            gated(c, first, count)
        for first in (128, 192):
            mixed(c, first, 64)

    loop(0, CHUNKS, rest)

    loop(1, ROW, lambda i: a1_copy(i).wait_recv())
    loop(1, COLUMN, lambda i: a2_copy(i).start())

    @pl.when(has_left)
    def _():
        ph_copy().wait_recv()

    @pl.when(jnp.logical_not(has_left))
    def _():
        ph_recv[...] = jnp.zeros_like(ph_recv)
        gx[0:LTAPS, :] = jnp.zeros((LTAPS, COLS), BF16)

    @pl.when(jnp.logical_not(has_right))
    def _():
        gmx[ROWS : ROWS + LTAPS, :] = jnp.zeros((LTAPS, COLS), BF16)
        gf_recv[...] = jnp.zeros_like(gf_recv)

    unfold(ph_recv, ph_stage, xs, EDGE - HALO)

    def edge(c):
        mixed(c, 0, EDGE)
        gated(c, 0, EDGE)

    loop(0, CHUNKS, edge)

    @pl.when(has_left)
    def _():
        gm0_copy().start()

    loads[6].wait()
    loads[7].wait()

    def own_spectra(q):
        for spec, values in ((spec_g, gx[LTAPS : LTAPS + ROWS, wide(q)]), (spec_gm, gmx[0:ROWS, wide(q)])):
            spec[:, wide(q)] = dot(fw[:, 0:ROWS], values) + dot(fw[:, 2 * ROWS : 3 * ROWS], values)

    loop(1, COLUMN, lambda i: b1_copy(i).wait_recv())
    loop(1, ROW, lambda i: b2_copy(i).start())

    loop(0, QUADS, own_spectra)

    def m_copy(q, i):
        return remote(
            gl_row_send.at[q, lax.rem(y + i, ROW)], gl_row_recv.at[q, i], msend.at[q, i], mrecv.at[q, i], in_row(i)
        )

    for q in range(QUADS):

        @pl.when(has_left)
        def _():
            g_copy(q).wait_recv()

        spec_g[:, WIDE * q : WIDE * (q + 1)] += dot(fw[:, ROWS : ROWS + LTAPS], gx[0:LTAPS, WIDE * q : WIDE * (q + 1)])
        for first in range(0, HALF, 64):
            re, im = pl.ds(first, 64), pl.ds(HALF + first, 64)
            cols = pl.ds(WIDE * q, WIDE)
            gc, gi = spec_g[re, cols], spec_g[im, cols]
            oc, oi = spec_gm[re, cols], spec_gm[im, cols]
            y1[re, :] = (oc * gc + oi * gi).astype(BF16)
            y1[im, :] = (oi * gc - oc * gi).astype(BF16)
        partial = dot(iv[ROWS:, :], y1[...]).astype(BF16)
        for row in range(ROW):
            gl_row_send[q, row] = partial[SHARE * row : SHARE * (row + 1), :]
        loop(1, ROW, lambda i: m_copy(q, i).start())

    @pl.when(has_right)
    def _():
        gm0_copy().wait_recv()

    for q in range(QUADS):

        @pl.when(has_right)
        def _():
            gm_copy(q).wait_recv()

        spec_gm[:, WIDE * q : WIDE * (q + 1)] -= dot(
            fw[:, ROWS : ROWS + LTAPS], gmx[ROWS : ROWS + LTAPS, WIDE * q : WIDE * (q + 1)]
        )

    loop(1, COLUMN, lambda i: a2_copy(i).wait_recv())
    loop(1, ROW, lambda i: b2_copy(i).wait_recv())

    for d in range(SEQ):
        dz, dy = divmod(d, ROW)
        fperm[0, 16 * d : 16 * (d + 1), :] = filt_a[dz, dy].astype(F32)
        fperm[1, 16 * d : 16 * (d + 1), :] = filt_b[dy, dz].astype(F32)

    for q in range(QUADS):
        parts = []
        for half in range(2):
            picked = [
                fperm[half, pl.ds(16 * first + OWN_TAPS * q + i, 8, stride=16), :]
                for i in range(OWN_TAPS)
                for first in range(0, SEQ, 8)
            ]
            parts.append(jnp.concatenate(picked, axis=0).astype(BF16))
        taps = jnp.concatenate(parts, axis=1)
        spec_h[:, WIDE * q : WIDE * (q + 1)] = dot(fw[:, ROWS + LTAPS : 2 * ROWS], taps) * (1.0 / HALF)

    def gf_copy():
        return remote(gf_send, gf_recv, gf_sem.at[0], gf_sem.at[1], left)

    my_piece = lax.rem(me + SEQ - FIRST_OWNER, SEQ)

    def owner(p):
        return lax.rem(p + FIRST_OWNER, SEQ)

    def s_copy(p):
        return remote(gs_part.at[p], gs_recv.at[me], ssend.at[p], srecv.at[me], owner(p))

    def s_arrival(i):
        return remote(gs_part.at[0], gs_recv.at[peer(i)], ssend.at[0], srecv.at[peer(i)], peer(i))

    def a_copy(d):
        return remote(gs_all.at[my_piece], gs_all.at[my_piece], asend.at[d], arecv.at[my_piece], d)

    def a_arrival(p):
        return remote(gs_all.at[p], gs_all.at[p], asend.at[0], arecv.at[p], owner(p))

    def short_grad(q, half):
        c = 2 * q + half
        for s in range(3):
            totals = [None] * STAPS
            for first in range(0, ROWS, 64):
                grad = fs[s, c, pl.ds(first, 64), :]
                for j in range(STAPS):
                    term = jnp.sum((grad * xs[s, c, pl.ds(EDGE + first - j, 64), :]).reshape(8, 8, LANES), axis=0)
                    totals[j] = term if totals[j] is None else totals[j] + term
            rows = jnp.concatenate([jnp.sum(t, axis=0, keepdims=True) for t in totals], axis=0)
            start = STAPS * (3 * half + s)
            gs_rows[q, start : start + STAPS, :] = rows

    def main(q):
        for first in range(0, HALF, 64):
            re, im = pl.ds(first, 64), pl.ds(HALF + first, 64)
            gc, gi = spec_g[re, wide(q)], spec_g[im, wide(q)]
            mc, mi = spec_gm[re, wide(q)], spec_gm[im, wide(q)]
            hc, hi = spec_h[re, wide(q)], spec_h[im, wide(q)]
            y1[re, :] = (gc * hc - gi * hi).astype(BF16)
            y1[im, :] = (gc * hi + gi * hc).astype(BF16)
            y2[re, :] = (mc * hc + mi * hi).astype(BF16)
            y2[im, :] = (mi * hc - mc * hi).astype(BF16)
        mixing = dot(iv[0:ROWS, :], y1[...])
        grad_gating = dot(iv[0:ROWS, :], y2[...])
        for half in range(2):
            c = 2 * q + half
            part = slice(half * LANES, (half + 1) * LANES)
            fs[0, c, 0:ROWS, :] = ov[:, lanes(c)].astype(F32) * mixing[:, part]
            fs[1, c, 0:ROWS, :] = grad_gating[:, part] * fkv[1, c]
            fs[2, c, 0:ROWS, :] = grad_gating[:, part] * fkv[0, c]

    def shorts(q):
        gs_rows[q, 40:48, :] = jnp.zeros((8, LANES), F32)
        for half in range(2):
            short_grad(q, half)

    def give(q):
        for k in range(3):
            piece = 3 * q + k
            gs_part[piece] = gs_rows[q, 16 * k : 16 * (k + 1), :].astype(BF16)

            @pl.when(piece != my_piece)
            def _():
                s_copy(piece).start()

            @pl.when(piece == my_piece)
            def _():
                gs_recv[me] = gs_part[piece]

    main(0)
    for q in range(1, QUADS):
        main(q)
        shorts(q - 1)
        give(q - 1)
    shorts(QUADS - 1)
    give(QUADS - 1)

    fold(gf_stage, fs, 0, gf_send)

    @pl.when(has_left)
    def _():
        gf_copy().start()

    def l_copy(i):
        return remote(gl_send.at[lax.rem(z + i, COLUMN)], gl_recv.at[i], lsend.at[i], lrecv.at[i], in_column(i))

    for q in range(QUADS):
        loop(1, ROW, lambda i: m_copy(q, i).wait_recv())
        total = gl_row_send[q, y].astype(F32)
        for i in range(1, ROW):
            total = total + gl_row_recv[q, i].astype(F32)
        for half in range(2):
            for i in range(OWN_TAPS):
                rows = total[COLUMN * i : COLUMN * (i + 1), half * LANES : (half + 1) * LANES]
                lperm[half, pl.ds(OWN_TAPS * q + i, COLUMN, stride=16), :] = rows
    for d in range(COLUMN):
        for half in range(2):
            gl_send[d, :, half * LANES : (half + 1) * LANES] = lperm[half, 16 * d : 16 * (d + 1), :].astype(BF16)
    loop(1, COLUMN, lambda i: l_copy(i).start())
    gl_recv[0] = gl_send[z]

    def back(c, first, count):
        for s in range(3):
            total = None
            for j in range(STAPS):
                term = sfv[s, j : j + 1, lanes(c)] * fs[s, c, pl.ds(first + j, count), :]
                total = term if total is None else total + term
            gp_v[s, pl.ds(first, count), lanes(c)] = total.astype(BF16)

    def back_bulk(c):
        for first, count in ((0, 64), (64, 64), (128, 64), (192, 48)):
            back(c, first, count)

    loop(0, CHUNKS, back_bulk)

    @pl.when(has_right)
    def _():
        gf_copy().wait_recv()

    unfold(gf_recv, gf_stage, fs, ROWS)

    def back_edge(c):
        back(c, ROWS - EDGE, EDGE)

    loop(0, CHUNKS, back_edge)

    def hand_out(d):
        @pl.when(d != me)
        def _():
            a_copy(d).start()

    @pl.when(my_piece < PIECES)
    def _():
        loop(1, SEQ, lambda i: s_arrival(i).wait_recv())
        total = gs_recv[0].astype(F32)
        for d in range(1, SEQ):
            total = total + gs_recv[d].astype(F32)
        gs_all[my_piece] = total.astype(BF16)
        loop(0, SEQ, hand_out)

    loop(1, COLUMN, lambda i: l_copy(i).wait_recv())
    total = gl_recv[0].astype(F32)
    for d in range(1, COLUMN):
        total = total + gl_recv[d].astype(F32)
    gl_sum[...] = total * (1.0 / HALF)
    for q in range(QUADS):
        gl_out[:, WIDE * q : WIDE * (q + 1)] = gl_sum[OWN_TAPS * q : OWN_TAPS * (q + 1), :]

    @pl.when(has_right)
    def _():
        ph_copy().wait_send()
        loop(0, QUADS, lambda q: g_copy(q).wait_send())

    @pl.when(has_left)
    def _():
        loop(0, QUADS, lambda q: gm_copy(q).wait_send())
        gm0_copy().wait_send()
        gf_copy().wait_send()

    for i in range(1, ROW):
        a1_copy(i).wait_send()
        b2_copy(i).wait_send()
    for i in range(1, COLUMN):
        a2_copy(i).wait_send()
        b1_copy(i).wait_send()
    loop(1, COLUMN, lambda i: l_copy(i).wait_send())
    for q in range(QUADS):
        loop(1, ROW, lambda i: m_copy(q, i).wait_send())

    def s_sent(p):
        @pl.when(p != my_piece)
        def _():
            s_copy(p).wait_send()

    loop(0, PIECES, s_sent)

    def a_sent(d):
        @pl.when(d != me)
        def _():
            a_copy(d).wait_send()

    @pl.when(my_piece < PIECES)
    def _():
        loop(0, SEQ, a_sent)

    def a_wait(p):
        @pl.when(p != my_piece)
        def _():
            a_arrival(p).wait_recv()

    loop(0, PIECES, a_wait)
    for q in range(QUADS):
        for k in range(3):
            gs_rows[q, 16 * k : 16 * (k + 1), :] = gs_all[3 * q + k].astype(F32)
        for half in range(2):
            for s in range(3):
                start, c = STAPS * (3 * half + s), 2 * q + half
                gs_out[s, :, c * LANES : (c + 1) * LANES] = gs_rows[q, start : start + STAPS, :]


def write_out(gp, gs, gl, gp_hbm, gs_hbm, gl_hbm, sems):
    copies = [pltpu.make_async_copy(src, dst, sems.at[n]) for n, (src, dst) in enumerate(((gp, gp_hbm), (gs, gs_hbm), (gl, gl_hbm)))]
    for copy in copies:
        copy.start()
    for copy in copies:
        copy.wait()


def on_device(projections, out_grad, short_filters, long_filter):
    forward, inverse = transforms()
    dma = pltpu.SemaphoreType.DMA
    vmem = pltpu.VMEM
    scratch = [
        vmem((3, ROWS, COLS), BF16),
        vmem((ROWS, COLS), BF16),
        vmem((3, STAPS, COLS), F32),
        vmem((OWN_TAPS, COLS), F32),
        vmem(forward.shape, BF16),
        vmem(inverse.shape, BF16),
        vmem((3, CHUNKS, EDGE + ROWS, LANES), F32),
        vmem((3, CHUNKS, ROWS + EDGE, LANES), F32),
        vmem((2, CHUNKS, ROWS, LANES), F32),
        vmem((LTAPS + ROWS, COLS), BF16),
        vmem((ROWS + LTAPS, COLS), BF16),
        vmem((CHUNKS + 1, EDGE, LANES), F32),
        vmem((EDGE, COLS + LANES), BF16),
        vmem((EDGE, COLS + LANES), BF16),
        vmem((CHUNKS + 1, EDGE, LANES), F32),
        vmem((EDGE, COLS + LANES), BF16),
        vmem((EDGE, COLS + LANES), BF16),
        vmem((COLUMN, ROW, 16, LANES), BF16),
        vmem((ROW, COLUMN, 16, LANES), BF16),
        vmem((2, SEQ * 16, LANES), F32),
        vmem((POINTS, COLS), F32),
        vmem((POINTS, COLS), F32),
        vmem((POINTS, COLS), F32),
        vmem((POINTS, WIDE), BF16),
        vmem((POINTS, WIDE), BF16),
        vmem((2, SEQ * 16, LANES), F32),
        vmem((QUADS, ROW, SHARE, WIDE), BF16),
        vmem((QUADS, ROW, SHARE, WIDE), BF16),
        vmem((COLUMN, 16, WIDE), BF16),
        vmem((COLUMN, 16, WIDE), BF16),
        vmem((16, WIDE), F32),
        vmem((QUADS, 48, LANES), F32),
        vmem((PIECES, 16, LANES), BF16),
        vmem((SEQ, 16, LANES), BF16),
        vmem((PIECES, 16, LANES), BF16),
        dma((8,)), dma((2,)), dma((2, QUADS)), dma((2, QUADS)), dma((2,)), dma((2,)),
        dma((SEQ,)), dma((SEQ,)), dma((QUADS, ROW)), dma((QUADS, ROW)), dma((COLUMN,)), dma((COLUMN,)), dma((PIECES,)), dma((SEQ,)), dma((SEQ,)), dma((SEQ,)),
    ]
    hbm = pl.BlockSpec(memory_space=pltpu.HBM)
    in_vmem = pl.BlockSpec(memory_space=pltpu.VMEM)
    operands = (projections, out_grad, short_filters, long_filter, jnp.asarray(forward), jnp.asarray(inverse))
    results = pl.pallas_call(
        kernel,
        out_shape=(
            pltpu.VMEM(projections.shape, BF16),
            pltpu.VMEM(short_filters.shape, F32),
            pltpu.VMEM(long_filter.shape, F32),
        ),
        in_specs=[hbm] * len(operands),
        out_specs=(in_vmem,) * 3,
        scratch_shapes=scratch,
        compiler_params=pltpu.CompilerParams(collective_id=0, has_side_effects=True, vmem_limit_bytes=50 << 20),
    )(*[pltpu.with_memory_space_constraint(operand, pltpu.HBM) for operand in operands])
    return pl.pallas_call(
        write_out,
        out_shape=tuple(jax.ShapeDtypeStruct(r.shape, r.dtype) for r in results),
        in_specs=[in_vmem] * 3,
        out_specs=(hbm,) * 3,
        scratch_shapes=[dma((3,))],
    )(*[pltpu.with_memory_space_constraint(result, pltpu.VMEM) for result in results])


def solution(mesh):
    in_specs = (
        P(None, "seq", "tensor"),
        P("seq", "tensor"),
        P(None, None, "tensor"),
        P("seq", "tensor"),
    )
    out_specs = (P(None, "seq", "tensor"), P(None, None, "tensor"), P("seq", "tensor"))
    return jax.shard_map(on_device, mesh=mesh, in_specs=in_specs, out_specs=out_specs, check_vma=False)
```

```python
import jax
import jax.numpy as jnp
import ml_dtypes
import numpy as np
from jax import lax
from jax.experimental import pallas as pl
from jax.experimental.pallas import tpu as pltpu
from jax.sharding import PartitionSpec as P

MESH = pl.DeviceIdType.MESH
F32 = jnp.float32
BF16 = jnp.bfloat16

STAPS = 7
LTAPS = 128
ROWS = 256
COLS = 1024
LANES = 128
CHUNKS = COLS // LANES
WIDE = 256
QUADS = COLS // WIDE
SEQ = 32
OWN_TAPS = LTAPS // SEQ
POINTS = ROWS + LTAPS
HALF = POINTS // 2
EDGE = 16
PIECES = 3 * QUADS
ROW = 4
COLUMN = 8
FIRST_OWNER = 30
HALO = STAPS - 1
SHARE = LTAPS // ROW


def transforms():
    freqs = 2.0 * np.pi * (np.arange(HALF) + 0.5) / POINTS

    def rows(times):
        angles = np.outer(freqs, times)
        return np.concatenate([np.cos(angles), np.sin(angles)], axis=0)

    own = rows(np.arange(ROWS))
    prior = rows(np.arange(-LTAPS, 0))
    tap_order = np.arange(LTAPS).reshape(SEQ, OWN_TAPS).T.reshape(-1)
    taps = rows(tap_order)
    own_rest = own - own.astype(ml_dtypes.bfloat16).astype(np.float64)
    forward = np.concatenate([own, prior, taps, own_rest], axis=1).astype(ml_dtypes.bfloat16)
    grad_order = np.arange(LTAPS).reshape(COLUMN, ROW, OWN_TAPS).transpose(1, 2, 0).reshape(-1)
    inverse = np.concatenate([own.T, rows(grad_order).T], axis=0).astype(ml_dtypes.bfloat16)
    return forward, inverse


def lanes(c):
    return pl.ds(pl.multiple_of(c * LANES, LANES), LANES)


def wide(q):
    return pl.ds(pl.multiple_of(q * WIDE, WIDE), WIDE)


def dot(a, b):
    return jnp.dot(a, b, preferred_element_type=F32)


def kernel(
    proj_hbm, og_hbm, sf_hbm, lf_hbm, fw_hbm, iv_hbm,
    gp_v, gs_out, gl_out,
    pv, ov, sfv, lfv, fw, iv,
    xs, fs, fkv, gx, gmx, ph_stage, ph_send, ph_recv, gf_stage, gf_send, gf_recv,
    filt_a, filt_b, fperm, spec_g, spec_gm, spec_h, y1, y2,
    lperm, gl_row_send, gl_row_recv, gl_send, gl_recv, gl_sum, gs_rows, gs_part, gs_recv, gs_all,
    load_sem, ph_sem, g_sem, gm_sem, gm0_sem, gf_sem,
    fsend, frecv, msend, mrecv, lsend, lrecv, ssend, srecv, asend, arecv,
):
    me = lax.axis_index("seq")
    right, left = lax.rem(me + 1, SEQ), lax.rem(me + SEQ - 1, SEQ)
    has_left, has_right = me > 0, me < SEQ - 1

    def peer(i):
        return lax.rem(me + i, SEQ)

    def remote(src, dst, send_sem, recv_sem, to):
        return pltpu.make_async_remote_copy(
            src_ref=src, dst_ref=dst, send_sem=send_sem, recv_sem=recv_sem,
            device_id={"seq": to}, device_id_type=MESH,
        )

    def loop(low, high, body):
        lax.fori_loop(low, high, lambda i, _: (body(i), 0)[1], 0)

    y, z = lax.rem(me, ROW), lax.div(me, ROW)

    def in_row(i):
        return z * ROW + lax.rem(y + i, ROW)

    def in_column(i):
        return lax.rem(z + i, COLUMN) * ROW + y

    barrier = pltpu.get_barrier_semaphore()
    greeted = [left, right] + [in_row(i) for i in range(1, ROW)] + [in_column(i) for i in range(1, COLUMN)]
    for other in greeted:
        pl.semaphore_signal(barrier, inc=1, device_id={"seq": other}, device_id_type=MESH)

    loads = [
        pltpu.make_async_copy(src, dst, load_sem.at[n])
        for n, (src, dst) in enumerate(
            [
                (sf_hbm, sfv), (proj_hbm.at[1], pv.at[1]), (proj_hbm.at[2], pv.at[2]), (proj_hbm.at[0], pv.at[0]),
                (og_hbm, ov), (lf_hbm, lfv), (fw_hbm, fw), (iv_hbm, iv),
            ]
        )
    ]
    for load in loads:
        load.start()

    def feature(s, c, first, count):
        total = None
        for j in range(STAPS):
            term = sfv[s, j : j + 1, lanes(c)] * xs[s, c, pl.ds(EDGE + first - j, count), :]
            total = term if total is None else total + term
        return total

    def gated(c, first, count):
        k, v = feature(1, c, first, count), feature(2, c, first, count)
        fkv[0, c, pl.ds(first, count), :] = k
        fkv[1, c, pl.ds(first, count), :] = v
        gx[pl.ds(LTAPS + first, count), lanes(c)] = (k * v).astype(BF16)

    def mixed(c, first, count):
        cotangent = ov[pl.ds(first, count), lanes(c)].astype(F32)
        gmx[pl.ds(first, count), lanes(c)] = (cotangent * feature(0, c, first, count)).astype(BF16)

    def widen(s, c):
        xs[s, c, pl.ds(EDGE, ROWS), :] = pv[s, :, lanes(c)].astype(F32)

    for load in loads[:3]:
        load.wait()

    def tail(c):
        widen(1, c)
        widen(2, c)
        for first in (128, 192):
            gated(c, first, 64)

    loop(0, CHUNKS, tail)
    loads[3].wait()
    loads[4].wait()

    def head(c):
        widen(0, c)
        for first, count in ((16, 48), (64, 64)):
            mixed(c, first, count)

    loop(0, CHUNKS, head)
    loads[5].wait()
    for q in range(QUADS):
        lperm[0, OWN_TAPS * q : OWN_TAPS * (q + 1), :] = lfv[:, WIDE * q : WIDE * q + LANES]
        lperm[1, OWN_TAPS * q : OWN_TAPS * (q + 1), :] = lfv[:, WIDE * q + LANES : WIDE * (q + 1)]
    filt_a[z, y] = lperm[0, 0:16, :].astype(BF16)
    filt_b[y, z] = lperm[1, 0:16, :].astype(BF16)

    def fold(stage, source, first, packed):
        for c in range(CHUNKS):
            stage[c, 0:6, :] = source[0, c, first : first + 6, :]
            stage[c, 6:12, :] = source[1, c, first : first + 6, :]
            stage[c, 12:16, :] = source[2, c, first : first + 4, :]
            stage[CHUNKS, 2 * c : 2 * c + 2, :] = source[2, c, first + 4 : first + 6, :]
        for c in range(CHUNKS + 1):
            packed[:, LANES * c : LANES * (c + 1)] = stage[c, 0:EDGE, :].astype(BF16)

    def unfold(packed, stage, target, first):
        for c in range(CHUNKS + 1):
            stage[c, 0:EDGE, :] = packed[:, LANES * c : LANES * (c + 1)].astype(F32)
        for c in range(CHUNKS):
            target[0, c, first : first + 6, :] = stage[c, 0:6, :]
            target[1, c, first : first + 6, :] = stage[c, 6:12, :]
            target[2, c, first : first + 4, :] = stage[c, 12:16, :]
            target[2, c, first + 4 : first + 6, :] = stage[CHUNKS, 2 * c : 2 * c + 2, :]

    fold(ph_stage, xs, EDGE + ROWS - HALO, ph_send)

    pl.semaphore_wait(barrier, len(greeted))

    def ph_copy():
        return remote(ph_send, ph_recv, ph_sem.at[0], ph_sem.at[1], right)

    def g_copy(q):
        return remote(gx.at[pl.ds(ROWS, LTAPS), wide(q)], gx.at[pl.ds(0, LTAPS), wide(q)], g_sem.at[0, q], g_sem.at[1, q], right)

    def gm_copy(q):
        return remote(
            gmx.at[pl.ds(EDGE, LTAPS - EDGE), wide(q)], gmx.at[pl.ds(ROWS + EDGE, LTAPS - EDGE), wide(q)],
            gm_sem.at[0, q], gm_sem.at[1, q], left,
        )

    def gm0_copy():
        return remote(gmx.at[pl.ds(0, EDGE), :], gmx.at[pl.ds(ROWS, EDGE), :], gm0_sem.at[0], gm0_sem.at[1], left)

    def a1_copy(i):
        return remote(filt_a.at[z, y], filt_a.at[z, y], fsend.at[i], frecv.at[i], in_row(i))

    def a2_copy(i):
        return remote(filt_a.at[z], filt_a.at[z], fsend.at[ROW + i], frecv.at[ROW + i], in_column(i))

    def b1_copy(i):
        return remote(filt_b.at[y, z], filt_b.at[y, z], fsend.at[12 + i], frecv.at[12 + i], in_column(i))

    def b2_copy(i):
        return remote(filt_b.at[y], filt_b.at[y], fsend.at[20 + i], frecv.at[20 + i], in_row(i))

    loop(1, ROW, lambda i: a1_copy(i).start())
    loop(1, COLUMN, lambda i: b1_copy(i).start())

    @pl.when(has_right)
    def _():
        ph_copy().start()
        loop(0, QUADS, lambda q: g_copy(q).start())

    @pl.when(has_left)
    def _():
        loop(0, QUADS, lambda q: gm_copy(q).start())

    def rest(c):
        for first, count in ((16, 48), (64, 64)):
            gated(c, first, count)
        for first in (128, 192):
            mixed(c, first, 64)

    loop(0, CHUNKS, rest)

    loop(1, ROW, lambda i: a1_copy(i).wait_recv())
    loop(1, COLUMN, lambda i: a2_copy(i).start())

    @pl.when(has_left)
    def _():
        ph_copy().wait_recv()

    @pl.when(jnp.logical_not(has_left))
    def _():
        ph_recv[...] = jnp.zeros_like(ph_recv)
        gx[0:LTAPS, :] = jnp.zeros((LTAPS, COLS), BF16)

    @pl.when(jnp.logical_not(has_right))
    def _():
        gmx[ROWS : ROWS + LTAPS, :] = jnp.zeros((LTAPS, COLS), BF16)
        gf_recv[...] = jnp.zeros_like(gf_recv)

    unfold(ph_recv, ph_stage, xs, EDGE - HALO)

    def edge(c):
        mixed(c, 0, EDGE)
        gated(c, 0, EDGE)

    loop(0, CHUNKS, edge)

    @pl.when(has_left)
    def _():
        gm0_copy().start()

    loads[6].wait()
    loads[7].wait()

    def own_spectra(q):
        for spec, values in ((spec_g, gx[LTAPS : LTAPS + ROWS, wide(q)]), (spec_gm, gmx[0:ROWS, wide(q)])):
            spec[:, wide(q)] = dot(fw[:, 0:ROWS], values) + dot(fw[:, 2 * ROWS : 3 * ROWS], values)

    loop(1, COLUMN, lambda i: b1_copy(i).wait_recv())
    loop(1, ROW, lambda i: b2_copy(i).start())

    loop(0, QUADS, own_spectra)

    def m_copy(q, i):
        return remote(
            gl_row_send.at[q, lax.rem(y + i, ROW)], gl_row_recv.at[q, i], msend.at[q, i], mrecv.at[q, i], in_row(i)
        )

    for q in range(QUADS):

        @pl.when(has_left)
        def _():
            g_copy(q).wait_recv()

        spec_g[:, WIDE * q : WIDE * (q + 1)] += dot(fw[:, ROWS : ROWS + LTAPS], gx[0:LTAPS, WIDE * q : WIDE * (q + 1)])
        for first in range(0, HALF, 64):
            re, im = pl.ds(first, 64), pl.ds(HALF + first, 64)
            cols = pl.ds(WIDE * q, WIDE)
            gc, gi = spec_g[re, cols], spec_g[im, cols]
            oc, oi = spec_gm[re, cols], spec_gm[im, cols]
            y1[re, :] = (oc * gc + oi * gi).astype(BF16)
            y1[im, :] = (oi * gc - oc * gi).astype(BF16)
        partial = dot(iv[ROWS:, :], y1[...]).astype(BF16)
        for row in range(ROW):
            gl_row_send[q, row] = partial[SHARE * row : SHARE * (row + 1), :]
        loop(1, ROW, lambda i: m_copy(q, i).start())

    @pl.when(has_right)
    def _():
        gm0_copy().wait_recv()

    for q in range(QUADS):

        @pl.when(has_right)
        def _():
            gm_copy(q).wait_recv()

        spec_gm[:, WIDE * q : WIDE * (q + 1)] -= dot(
            fw[:, ROWS : ROWS + LTAPS], gmx[ROWS : ROWS + LTAPS, WIDE * q : WIDE * (q + 1)]
        )

    loop(1, COLUMN, lambda i: a2_copy(i).wait_recv())
    loop(1, ROW, lambda i: b2_copy(i).wait_recv())

    for d in range(SEQ):
        dz, dy = divmod(d, ROW)
        fperm[0, 16 * d : 16 * (d + 1), :] = filt_a[dz, dy].astype(F32)
        fperm[1, 16 * d : 16 * (d + 1), :] = filt_b[dy, dz].astype(F32)

    for q in range(QUADS):
        parts = []
        for half in range(2):
            picked = [
                fperm[half, pl.ds(16 * first + OWN_TAPS * q + i, 8, stride=16), :]
                for i in range(OWN_TAPS)
                for first in range(0, SEQ, 8)
            ]
            parts.append(jnp.concatenate(picked, axis=0).astype(BF16))
        taps = jnp.concatenate(parts, axis=1)
        spec_h[:, WIDE * q : WIDE * (q + 1)] = dot(fw[:, ROWS + LTAPS : 2 * ROWS], taps) * (1.0 / HALF)

    def gf_copy():
        return remote(gf_send, gf_recv, gf_sem.at[0], gf_sem.at[1], left)

    my_piece = lax.rem(me + SEQ - FIRST_OWNER, SEQ)

    def owner(p):
        return lax.rem(p + FIRST_OWNER, SEQ)

    def s_copy(p):
        return remote(gs_part.at[p], gs_recv.at[me], ssend.at[p], srecv.at[me], owner(p))

    def s_arrival(i):
        return remote(gs_part.at[0], gs_recv.at[peer(i)], ssend.at[0], srecv.at[peer(i)], peer(i))

    def a_copy(d):
        return remote(gs_all.at[my_piece], gs_all.at[my_piece], asend.at[d], arecv.at[my_piece], d)

    def a_arrival(p):
        return remote(gs_all.at[p], gs_all.at[p], asend.at[0], arecv.at[p], owner(p))

    def short_grad(q, half):
        c = 2 * q + half
        for s in range(3):
            totals = [None] * STAPS
            for first in range(0, ROWS, 64):
                grad = fs[s, c, pl.ds(first, 64), :]
                for j in range(STAPS):
                    term = jnp.sum((grad * xs[s, c, pl.ds(EDGE + first - j, 64), :]).reshape(8, 8, LANES), axis=0)
                    totals[j] = term if totals[j] is None else totals[j] + term
            rows = jnp.concatenate([jnp.sum(t, axis=0, keepdims=True) for t in totals], axis=0)
            start = STAPS * (3 * half + s)
            gs_rows[q, start : start + STAPS, :] = rows

    def main(q):
        for first in range(0, HALF, 64):
            re, im = pl.ds(first, 64), pl.ds(HALF + first, 64)
            gc, gi = spec_g[re, wide(q)], spec_g[im, wide(q)]
            mc, mi = spec_gm[re, wide(q)], spec_gm[im, wide(q)]
            hc, hi = spec_h[re, wide(q)], spec_h[im, wide(q)]
            y1[re, :] = (gc * hc - gi * hi).astype(BF16)
            y1[im, :] = (gc * hi + gi * hc).astype(BF16)
            y2[re, :] = (mc * hc + mi * hi).astype(BF16)
            y2[im, :] = (mi * hc - mc * hi).astype(BF16)
        mixing = dot(iv[0:ROWS, :], y1[...])
        grad_gating = dot(iv[0:ROWS, :], y2[...])
        for half in range(2):
            c = 2 * q + half
            part = slice(half * LANES, (half + 1) * LANES)
            fs[0, c, 0:ROWS, :] = ov[:, lanes(c)].astype(F32) * mixing[:, part]
            fs[1, c, 0:ROWS, :] = grad_gating[:, part] * fkv[1, c]
            fs[2, c, 0:ROWS, :] = grad_gating[:, part] * fkv[0, c]

    def shorts(q):
        gs_rows[q, 40:48, :] = jnp.zeros((8, LANES), F32)
        for half in range(2):
            short_grad(q, half)

    def give(q):
        for k in range(3):
            piece = 3 * q + k
            gs_part[piece] = gs_rows[q, 16 * k : 16 * (k + 1), :].astype(BF16)

            @pl.when(piece != my_piece)
            def _():
                s_copy(piece).start()

            @pl.when(piece == my_piece)
            def _():
                gs_recv[me] = gs_part[piece]

    main(0)
    for q in range(1, QUADS):
        main(q)
        shorts(q - 1)
        give(q - 1)
    shorts(QUADS - 1)
    give(QUADS - 1)

    fold(gf_stage, fs, 0, gf_send)

    @pl.when(has_left)
    def _():
        gf_copy().start()

    def l_copy(i):
        return remote(gl_send.at[lax.rem(z + i, COLUMN)], gl_recv.at[i], lsend.at[i], lrecv.at[i], in_column(i))

    for q in range(QUADS):
        loop(1, ROW, lambda i: m_copy(q, i).wait_recv())
        total = gl_row_send[q, y].astype(F32)
        for i in range(1, ROW):
            total = total + gl_row_recv[q, i].astype(F32)
        for half in range(2):
            for i in range(OWN_TAPS):
                rows = total[COLUMN * i : COLUMN * (i + 1), half * LANES : (half + 1) * LANES]
                lperm[half, pl.ds(OWN_TAPS * q + i, COLUMN, stride=16), :] = rows
    for d in range(COLUMN):
        for half in range(2):
            gl_send[d, :, half * LANES : (half + 1) * LANES] = lperm[half, 16 * d : 16 * (d + 1), :].astype(BF16)
    loop(1, COLUMN, lambda i: l_copy(i).start())
    gl_recv[0] = gl_send[z]

    def back(c, first, count):
        for s in range(3):
            total = None
            for j in range(STAPS):
                term = sfv[s, j : j + 1, lanes(c)] * fs[s, c, pl.ds(first + j, count), :]
                total = term if total is None else total + term
            gp_v[s, pl.ds(first, count), lanes(c)] = total.astype(BF16)

    def back_bulk(c):
        for first, count in ((0, 64), (64, 64), (128, 64), (192, 48)):
            back(c, first, count)

    loop(0, CHUNKS, back_bulk)

    @pl.when(has_right)
    def _():
        gf_copy().wait_recv()

    unfold(gf_recv, gf_stage, fs, ROWS)

    def back_edge(c):
        back(c, ROWS - EDGE, EDGE)

    loop(0, CHUNKS, back_edge)

    def hand_out(d):
        @pl.when(d != me)
        def _():
            a_copy(d).start()

    @pl.when(my_piece < PIECES)
    def _():
        loop(1, SEQ, lambda i: s_arrival(i).wait_recv())
        total = gs_recv[0].astype(F32)
        for d in range(1, SEQ):
            total = total + gs_recv[d].astype(F32)
        gs_all[my_piece] = total.astype(BF16)
        loop(0, SEQ, hand_out)

    loop(1, COLUMN, lambda i: l_copy(i).wait_recv())
    total = gl_recv[0].astype(F32)
    for d in range(1, COLUMN):
        total = total + gl_recv[d].astype(F32)
    gl_sum[0:16, :] = total * (1.0 / HALF)
    for q in range(QUADS):
        gl_out[:, WIDE * q : WIDE * (q + 1)] = gl_sum[OWN_TAPS * q : OWN_TAPS * (q + 1), :]

    @pl.when(has_right)
    def _():
        ph_copy().wait_send()
        loop(0, QUADS, lambda q: g_copy(q).wait_send())

    @pl.when(has_left)
    def _():
        loop(0, QUADS, lambda q: gm_copy(q).wait_send())
        gm0_copy().wait_send()
        gf_copy().wait_send()

    for i in range(1, ROW):
        a1_copy(i).wait_send()
        b2_copy(i).wait_send()
    for i in range(1, COLUMN):
        a2_copy(i).wait_send()
        b1_copy(i).wait_send()
    loop(1, COLUMN, lambda i: l_copy(i).wait_send())
    for q in range(QUADS):
        loop(1, ROW, lambda i: m_copy(q, i).wait_send())

    def s_sent(p):
        @pl.when(p != my_piece)
        def _():
            s_copy(p).wait_send()

    loop(0, PIECES, s_sent)

    def a_sent(d):
        @pl.when(d != me)
        def _():
            a_copy(d).wait_send()

    @pl.when(my_piece < PIECES)
    def _():
        loop(0, SEQ, a_sent)

    def a_wait(p):
        @pl.when(p != my_piece)
        def _():
            a_arrival(p).wait_recv()

    loop(0, PIECES, a_wait)
    for q in range(QUADS):
        for k in range(3):
            gs_rows[q, 16 * k : 16 * (k + 1), :] = gs_all[3 * q + k].astype(F32)
        for half in range(2):
            for s in range(3):
                start, c = STAPS * (3 * half + s), 2 * q + half
                gs_out[s, :, c * LANES : (c + 1) * LANES] = gs_rows[q, start : start + STAPS, :]


def write_out(gp, gs, gl, gp_hbm, gs_hbm, gl_hbm, sems):
    copies = [pltpu.make_async_copy(src, dst, sems.at[n]) for n, (src, dst) in enumerate(((gp, gp_hbm), (gs, gs_hbm), (gl, gl_hbm)))]
    for copy in copies:
        copy.start()
    for copy in copies:
        copy.wait()


def on_device(projections, out_grad, short_filters, long_filter):
    forward, inverse = transforms()
    dma = pltpu.SemaphoreType.DMA
    vmem = pltpu.VMEM
    scratch = [
        vmem((3, ROWS, COLS), BF16),
        vmem((ROWS, COLS), BF16),
        vmem((3, STAPS, COLS), F32),
        vmem((OWN_TAPS, COLS), F32),
        vmem(forward.shape, BF16),
        vmem(inverse.shape, BF16),
        vmem((3, CHUNKS, EDGE + ROWS, LANES), F32),
        vmem((3, CHUNKS, ROWS + EDGE, LANES), F32),
        vmem((2, CHUNKS, ROWS, LANES), F32),
        vmem((LTAPS + ROWS, COLS), BF16),
        vmem((ROWS + LTAPS, COLS), BF16),
        vmem((CHUNKS + 1, EDGE + 8, LANES), F32),
        vmem((EDGE, COLS + LANES), BF16),
        vmem((EDGE, COLS + LANES), BF16),
        vmem((CHUNKS + 1, EDGE + 8, LANES), F32),
        vmem((EDGE, COLS + LANES), BF16),
        vmem((EDGE, COLS + LANES), BF16),
        vmem((COLUMN, ROW, 16, LANES), BF16),
        vmem((ROW, COLUMN, 16, LANES), BF16),
        vmem((2, SEQ * 16 + LANES, LANES), F32),
        vmem((POINTS, COLS), F32),
        vmem((POINTS, COLS), F32),
        vmem((POINTS, COLS), F32),
        vmem((POINTS, WIDE), BF16),
        vmem((POINTS, WIDE), BF16),
        vmem((2, SEQ * 16 + LANES, LANES), F32),
        vmem((QUADS, ROW, SHARE, WIDE), BF16),
        vmem((QUADS, ROW, SHARE, WIDE), BF16),
        vmem((COLUMN, 16, WIDE), BF16),
        vmem((COLUMN, 16, WIDE), BF16),
        vmem((24, WIDE), F32),
        vmem((QUADS, 56, LANES), F32),
        vmem((PIECES, 16, LANES), BF16),
        vmem((SEQ, 16, LANES), BF16),
        vmem((PIECES, 16, LANES), BF16),
        dma((8,)), dma((2,)), dma((2, QUADS)), dma((2, QUADS)), dma((2,)), dma((2,)),
        dma((SEQ,)), dma((SEQ,)), dma((QUADS, ROW)), dma((QUADS, ROW)), dma((COLUMN,)), dma((COLUMN,)), dma((PIECES,)), dma((SEQ,)), dma((SEQ,)), dma((SEQ,)),
    ]
    hbm = pl.BlockSpec(memory_space=pltpu.HBM)
    in_vmem = pl.BlockSpec(memory_space=pltpu.VMEM)
    operands = (projections, out_grad, short_filters, long_filter, jnp.asarray(forward), jnp.asarray(inverse))
    results = pl.pallas_call(
        kernel,
        out_shape=(
            pltpu.VMEM(projections.shape, BF16),
            pltpu.VMEM(short_filters.shape, F32),
            pltpu.VMEM(long_filter.shape, F32),
        ),
        in_specs=[hbm] * len(operands),
        out_specs=(in_vmem,) * 3,
        scratch_shapes=scratch,
        compiler_params=pltpu.CompilerParams(collective_id=0, has_side_effects=True, vmem_limit_bytes=50 << 20),
    )(*[pltpu.with_memory_space_constraint(operand, pltpu.HBM) for operand in operands])
    return pl.pallas_call(
        write_out,
        out_shape=tuple(jax.ShapeDtypeStruct(r.shape, r.dtype) for r in results),
        in_specs=[in_vmem] * 3,
        out_specs=(hbm,) * 3,
        scratch_shapes=[dma((3,))],
    )(*[pltpu.with_memory_space_constraint(result, pltpu.VMEM) for result in results])


def solution(mesh):
    in_specs = (
        P(None, "seq", "tensor"),
        P("seq", "tensor"),
        P(None, None, "tensor"),
        P("seq", "tensor"),
    )
    out_specs = (P(None, "seq", "tensor"), P(None, None, "tensor"), P("seq", "tensor"))
    return jax.shard_map(on_device, mesh=mesh, in_specs=in_specs, out_specs=out_specs, check_vma=False)
```
